512 devices in a mesh: group: 16 (over z, core), dom: 32 (over y, x).
Axes of the slice: x: 4, y: 8, z: 8, core: 2. Of those that a mesh axis runs over, the one named last changes fastest.
Arguments:
- state: float32 [5, 393216], P(None, ('group', 'dom')), may hold values from -0.5 to 1.6, as said below
- pinv: bfloat16 [20, 40, 393216], P(None, None, ('group', 'dom')), may hold values from -0.21875 to 0.21875
- stencil: int32 [40, 393216], P(None, ('group', 'dom')), may hold values from 0 to 3071, as said below
- send_ids: int32 [16384, 64], P(('group', 'dom')), may hold values from 0 to 767
- group_ids: int32 [1024, 128], P(('group', 'dom')), may hold values from 0 to 767
- face_cells: int32 [2, 786432], P(None, ('group', 'dom')), may hold values from 0 to 3007, as said below
- face_geom: float32 [4, 786432], P(None, ('group', 'dom')), may hold values from -1 to 1, as said below
- face_basis: bfloat16 [80, 786432], P(None, ('group', 'dom')), may hold values from -3 to 3
Outputs:
- residual: float32 [5, 393216], P(None, ('group', 'dom'))
The draws below stay inside these ranges and needn't reach their ends.
Inputs may be any that keep to these rules, and one draw needn't show every extreme that they name: `stencil`: for a cell of partition g * 32 + d every entry is an own cell, or a column 768 + p * 64 + q where p differs from d in exactly one bit, or a column of the lower group block only if g > 0, of the upper only if g < 15. `face_cells`: row 0 is an own cell; row 1 is another own cell or a column that a stencil of the same partition may read, within the first 32 slots of a block of the same group or the first 64 slots of a group block. `face_geom`: rows 0 to 2 form a unit normal; row 3 is the area, from 0.2 to 1. `state`: density and pressure from 0.6 to 1.6, velocity components from -0.5 to 0.5.
All inputs are finite; a program needn't handle non-finite values.
Results may differ from the reference program's by a relative error of at most 0.0022.
Values sent between devices are 32-bit elements; how exact they have to be, the bound alone decides.
A program may use at most 64 MiB of HBM per device.

```python
import math
import jax
import jax.numpy as jnp
from jax import lax

COEF = 20
STEN = 40
POINTS = 2
CELLS_DEV = 768
CAP = 64
GCAP = 128
FACES_DEV = 1536
CELLS = 393216
FACES = 786432
N_GROUP = 16
N_DOM = 32
DEVICES = 512


def table_slots(key, count, width, half):
    shape = (DEVICES, count, width)
    levels = N_DOM.bit_length() - 1
    kinds = levels + 2
    device = jnp.arange(DEVICES, dtype=jnp.int32)[:, None, None]
    group = device // N_DOM
    column = device % N_DOM
    keys = jax.random.split(key, 4)
    source = jax.random.randint(keys[0], shape, 0, kinds)
    is_dom = source < levels
    is_low = source == levels
    flips = jnp.left_shift(jnp.ones_like(source), jnp.where(is_dom, source, 0))
    peer = jnp.bitwise_xor(column, flips)
    valid = jnp.where(is_dom, True, jnp.where(is_low, group > 0, group < N_GROUP - 1))
    block_sizes = jnp.where(jnp.arange(kinds, dtype=jnp.int32) < levels, CAP, GCAP)
    limits = jax.random.randint(keys[1], (DEVICES, kinds), block_sizes // 2, block_sizes + 1)
    if half:
        limits = jnp.broadcast_to(block_sizes // 2, (DEVICES, kinds))
    limit = jnp.take_along_axis(limits, source.reshape(DEVICES, -1), axis=1).reshape(shape)
    slot = jax.random.randint(keys[2], shape, 0, limit)
    base = jnp.where(is_dom, CELLS_DEV + peer * CAP, jnp.where(is_low, CELLS_DEV + N_DOM * CAP, CELLS_DEV + N_DOM * CAP + GCAP))
    chosen = (jax.random.randint(keys[3], shape, 0, 2) == 1) & valid
    return (chosen, base + slot)


def draw_stencil(key, part):
    key = jax.random.fold_in(key, 3)
    first, second = jax.random.split(key)
    chosen, ghost = table_slots(first, 40, CELLS_DEV, False)
    own = jax.random.randint(second, (DEVICES, 40, CELLS_DEV), 0, CELLS_DEV)
    slots = jnp.where(chosen, ghost, own)
    return slots.transpose(1, 0, 2).reshape(40, CELLS).astype(jnp.int32)


def draw_face_cells(key, part):
    key = jax.random.fold_in(key, 7)
    first, second, third = jax.random.split(key, 3)
    left = jax.random.randint(first, (DEVICES, 1, FACES_DEV), 0, CELLS_DEV)
    other = (left + 1 + jax.random.randint(second, (DEVICES, 1, FACES_DEV), 0, CELLS_DEV - 1)) % CELLS_DEV
    chosen, ghost = table_slots(third, 1, FACES_DEV, True)
    right = jnp.where(chosen, ghost, other)
    return jnp.concatenate([left.reshape(1, FACES), right.reshape(1, FACES)], axis=0).astype(jnp.int32)


def draw_face_geom(key, part):
    key = jax.random.fold_in(key, 11)
    first, second, third = jax.random.split(key, 3)
    polar = jnp.arccos(jax.random.uniform(first, (FACES,), jnp.float32, -1.0, 1.0))
    azimuth = jax.random.uniform(second, (FACES,), jnp.float32, -math.pi, math.pi)
    area = jnp.exp(jax.random.uniform(third, (FACES,), jnp.float32, math.log(0.2), 0.0))
    geom = jnp.stack([jnp.sin(polar) * jnp.cos(azimuth), jnp.sin(polar) * jnp.sin(azimuth), jnp.cos(polar), area], axis=0)
    return jnp.clip(geom, -1.0, 1.0).astype(jnp.float32)


def draw_state(key, part):
    key = jax.random.fold_in(key, 5)
    raw = jax.random.uniform(key, (5, CELLS), jnp.float32)
    lower = jnp.array([0.6, -0.5, -0.5, -0.5, 0.6], jnp.float32)[:, None]
    upper = jnp.array([1.6, 0.5, 0.5, 0.5, 1.6], jnp.float32)[:, None]
    return (lower + (upper - lower) * raw).astype(jnp.float32)


def place_ends(values, stream_key, least, largest):
    place = [jax.random.randint(jax.random.fold_in(stream_key, axis), (), 0, length) for axis, length in enumerate(values.shape)]
    longest = values.shape.index(max(values.shape))
    next_to = place[:longest] + [(place[longest] + 1) % values.shape[longest]] + place[longest + 1:]
    return values.at[tuple(place)].set(least).at[tuple(next_to)].set(largest)


def block_levels(rng, dims, pieces, low, high):
    def one(position, blocks):
        steps = jax.random.uniform(jax.random.fold_in(jax.random.fold_in(rng, 6), position), (blocks,), jnp.float32, low / len(pieces), high / len(pieces))
        return jnp.repeat(jnp.exp(steps), dims[position] // blocks).reshape((-1,) + (1,) * (len(dims) - position - 1))

    gain = one(*pieces[0])
    for cut in pieces[1:]:
        gain = gain * one(*cut)
    return gain


def normal_values(stream_key, dims, spread, most, cuts=(), kind=jnp.bfloat16):
    values = spread * jax.random.normal(stream_key, dims, jnp.float32)
    if cuts:
        values = values * block_levels(stream_key, dims, cuts, -0.22, 0.18)
    return jnp.clip(values, -most, most).astype(kind)


def setup_inputs(seed: int = 0) -> dict:
    key_list = jax.random.split(jax.random.key(seed), 9)
    return {
        "state": draw_state(jax.random.fold_in(key_list[8], 71), 0),
        "pinv": normal_values(key_list[1], (COEF, STEN, CELLS), (COEF * STEN) ** -0.5, 0.21875, ((2, 512),)),
        "stencil": draw_stencil(jax.random.fold_in(key_list[8], 71), 0),
        "send_ids": place_ends(jax.random.randint(key_list[3], (DEVICES * N_DOM, CAP), 0, CELLS_DEV), jax.random.fold_in(key_list[3], 1), 0, CELLS_DEV - 1).astype(jnp.int32),
        "group_ids": place_ends(jax.random.randint(key_list[4], (2 * DEVICES, GCAP), 0, CELLS_DEV), jax.random.fold_in(key_list[4], 1), 0, CELLS_DEV - 1).astype(jnp.int32),
        "face_cells": draw_face_cells(jax.random.fold_in(key_list[8], 71), 0),
        "face_geom": draw_face_geom(jax.random.fold_in(key_list[8], 71), 0),
        "face_basis": normal_values(key_list[7], (2 * POINTS * COEF, FACES), 1.0, 3.0, ((1, 512),)),
    }


GAMMA = 1.4
FLOOR = 0.2

def physical_flux(rho, velocity, pressure, normal):
    normal_speed = lax.optimization_barrier(jnp.sum(velocity * normal, axis=0))
    energy = (GAMMA / (GAMMA - 1.0) * pressure + 0.5 * rho * lax.optimization_barrier(jnp.sum(velocity * velocity, axis=0))) * normal_speed
    momentum = rho * velocity * normal_speed + pressure * normal
    return jnp.concatenate([(rho * normal_speed)[None], momentum, energy[None]], axis=0)

def entropy_fixed(eigen, sound):
    delta = 0.1 * sound
    magnitude = jnp.abs(eigen)
    return jnp.where(magnitude < delta, (eigen * eigen + delta * delta) / (2.0 * delta), magnitude)

def roe_flux(left, right, normal):
    rho_left, vel_left, pres_left = (left[0], left[1:4], left[4])
    rho_right, vel_right, pres_right = (right[0], right[1:4], right[4])
    root_left = jnp.sqrt(rho_left)
    root_right = jnp.sqrt(rho_right)
    weights = root_left + root_right
    rho_avg = root_left * root_right
    vel_avg = (root_left * vel_left + root_right * vel_right) / weights
    enth_left = GAMMA / (GAMMA - 1.0) * pres_left / rho_left + 0.5 * lax.optimization_barrier(jnp.sum(vel_left * vel_left, axis=0))
    enth_right = GAMMA / (GAMMA - 1.0) * pres_right / rho_right + 0.5 * lax.optimization_barrier(jnp.sum(vel_right * vel_right, axis=0))
    enth_avg = (root_left * enth_left + root_right * enth_right) / weights
    speed_sq = lax.optimization_barrier(jnp.sum(vel_avg * vel_avg, axis=0))
    sound_sq = (GAMMA - 1.0) * (enth_avg - 0.5 * speed_sq)
    sound = jnp.sqrt(sound_sq)
    normal_avg = lax.optimization_barrier(jnp.sum(vel_avg * normal, axis=0))
    d_rho = rho_right - rho_left
    d_pres = pres_right - pres_left
    d_vel = vel_right - vel_left
    d_normal = lax.optimization_barrier(jnp.sum(d_vel * normal, axis=0))
    wave_one = entropy_fixed(normal_avg - sound, sound) * (d_pres - rho_avg * sound * d_normal) / (2.0 * sound_sq)
    wave_five = entropy_fixed(normal_avg + sound, sound) * (d_pres + rho_avg * sound * d_normal) / (2.0 * sound_sq)
    middle = entropy_fixed(normal_avg, sound)
    wave_two = middle * (d_rho - d_pres / sound_sq)
    ones = jnp.ones_like(rho_avg)
    first = jnp.concatenate([ones[None], vel_avg - sound * normal, (enth_avg - sound * normal_avg)[None]], axis=0)
    second = jnp.concatenate([ones[None], vel_avg, (0.5 * speed_sq)[None]], axis=0)
    shear = jnp.concatenate([jnp.zeros_like(rho_avg)[None], d_vel - d_normal * normal, (lax.optimization_barrier(jnp.sum(vel_avg * d_vel, axis=0)) - normal_avg * d_normal)[None]], axis=0)
    fifth = jnp.concatenate([ones[None], vel_avg + sound * normal, (enth_avg + sound * normal_avg)[None]], axis=0)
    dissipation = wave_one * first + wave_two * second + middle * rho_avg * shear + wave_five * fifth
    total = physical_flux(rho_left, vel_left, pres_left, normal) + physical_flux(rho_right, vel_right, pres_right, normal)
    return 0.5 * total - 0.5 * dissipation

def floored(values):
    return jnp.concatenate([jnp.maximum(values[0:1], FLOOR), values[1:4], jnp.maximum(values[4:5], FLOOR)], axis=0)

def face_residual(value_table, coef_table, face_cells, face_geom, face_basis, count):
    faces = face_cells.shape[1]
    basis = face_basis.astype(jnp.float32).reshape(2, 2, 20, faces)
    normal = face_geom[0:3]
    area = face_geom[3]
    sides = []
    for side in range(2):
        slots = face_cells[side]
        centre = jnp.take(value_table, slots, axis=1)
        terms = jnp.take(coef_table, slots, axis=1).reshape(5, 20, faces)
        points = []
        for point in range(2):
            points.append(floored(centre + lax.optimization_barrier(jnp.sum(terms * basis[side, point][None], axis=1))))
        sides.append(points)
    flux = roe_flux(sides[0][0], sides[1][0], normal) + roe_flux(sides[0][1], sides[1][1], normal)
    weighted = (0.5 * area * flux).T
    right = face_cells[1]
    gained = jax.ops.segment_sum(weighted, face_cells[0], count)
    lost = jax.ops.segment_sum(weighted, jnp.where(right < count, right, count), count + 1)[:count]
    return (gained - lost).T

def ghost_slots(send_ids, group_ids, device):
    group = device // N_DOM
    column = device % N_DOM
    sends = send_ids.reshape(DEVICES, N_DOM, CAP)
    blocks = lax.dynamic_slice(sends, (group * N_DOM, column, column * 0), (N_DOM, 1, CAP))[:, 0, :]
    sources = group * N_DOM + jnp.arange(N_DOM, dtype=jnp.int32)
    dom_cells = (sources[:, None] * CELLS_DEV + blocks).reshape(-1)
    lists = group_ids.reshape(DEVICES, 2, GCAP)
    lower = jnp.maximum(group - 1, 0) * N_DOM + column
    upper = jnp.minimum(group + 1, N_GROUP - 1) * N_DOM + column
    low_cells = lower * CELLS_DEV + lists[lower, 0]
    high_cells = upper * CELLS_DEV + lists[upper, 1]
    return (dom_cells, low_cells, high_cells, group > 0, group < N_GROUP - 1)

def build_table(flat, own, slots):
    dom_cells, low_cells, high_cells, has_low, has_high = slots
    beside = jnp.take(flat, dom_cells, axis=1)
    lower = jnp.where(has_low, jnp.take(flat, low_cells, axis=1), jnp.zeros((), flat.dtype))
    upper = jnp.where(has_high, jnp.take(flat, high_cells, axis=1), jnp.zeros((), flat.dtype))
    return jnp.concatenate([own, beside, lower, upper], axis=1)

def reference(state, pinv, stencil, send_ids, group_ids, face_cells, face_geom, face_basis):
    devices = jnp.arange(DEVICES, dtype=jnp.int32)

    def coef_one(device):
        slots = ghost_slots(send_ids, group_ids, device)
        own = lax.dynamic_slice_in_dim(state, device * CELLS_DEV, CELLS_DEV, 1)
        table = build_table(state, own, slots)
        cells_stencil = lax.dynamic_slice_in_dim(stencil, device * CELLS_DEV, CELLS_DEV, 1)
        blocks = lax.dynamic_slice_in_dim(pinv, device * CELLS_DEV, CELLS_DEV, 2)
        near = jnp.take(table, cells_stencil, axis=1)
        diffs = (near - own[:, None, :]).astype(jnp.bfloat16)
        coefs = jnp.einsum('kjc,vjc->vkc', blocks.astype(jnp.float32), diffs.astype(jnp.float32))
        return coefs.reshape(100, CELLS_DEV)
    coefs = lax.map(coef_one, devices)
    coef_flat = coefs.transpose(1, 0, 2).reshape(100, CELLS)

    def residual_one(device):
        slots = ghost_slots(send_ids, group_ids, device)
        own = lax.dynamic_slice_in_dim(state, device * CELLS_DEV, CELLS_DEV, 1)
        own_coefs = lax.dynamic_slice_in_dim(coef_flat, device * CELLS_DEV, CELLS_DEV, 1)
        value_table = build_table(state, own, slots)
        coef_table = build_table(coef_flat, own_coefs, slots)
        cells_faces = lax.dynamic_slice_in_dim(face_cells, device * FACES_DEV, FACES_DEV, 1)
        geom = lax.dynamic_slice_in_dim(face_geom, device * FACES_DEV, FACES_DEV, 1)
        basis = lax.dynamic_slice_in_dim(face_basis, device * FACES_DEV, FACES_DEV, 1)
        return face_residual(value_table, coef_table, cells_faces, geom, basis, CELLS_DEV)
    result = lax.map(residual_one, devices)
    return result.transpose(1, 0, 2).reshape(5, CELLS)
```

```python
import functools

import jax
import jax.numpy as jnp
from jax import lax
from jax.experimental import pallas as pl
from jax.experimental.pallas import tpu as pltpu
from jax.sharding import PartitionSpec as P

GAMMA = 1.4
FLOOR = 0.2
MESH = pl.DeviceIdType.MESH
F32 = jnp.float32
BF16 = jnp.bfloat16
I32 = jnp.int32

CELLS = 768
FACES = 1536
CT = CELLS // 128
FT = FACES // 128
COEF = 20
STEN = 40
JT = STEN // 8
ROWS = 13
BITS = 5
UT = FT // 4


def loop(count, body):
    def step(i, carry):
        body(i)
        return carry

    lax.fori_loop(0, count, step, 0)


def lanes_at(tile):
    return pl.ds(pl.multiple_of(tile * 128, 128), 128)


def lane_gather(values, lanes):
    return jnp.take_along_axis(values, lanes, axis=1, mode="promise_in_bounds")


def wide(row):
    return jnp.broadcast_to(row, (8, 128))


def iota(axis):
    return lax.broadcasted_iota(I32, (8, 128), axis)


def merged(first, second, distance):
    mask = (iota(0) & distance) == 0
    kept = jnp.where(mask, first, second)
    moved = jnp.where(mask, second, first)
    return kept + pltpu.roll(moved, distance, 0)


def row_sums(parts):
    for distance in (1, 2, 4):
        parts = [merged(parts[i], parts[i + 1], distance) for i in range(0, len(parts), 2)]
    return parts[0]


def selected(tiles, lanes, tile, start, acc):
    for i, values in enumerate(tiles):
        got = lane_gather(values, lanes)
        acc = got if acc is None else jnp.where(tile == start + i, got, acc)
    return acc


def table_index(slot, column):
    flip = lax.shift_right_arithmetic(slot - 768, 6) ^ column
    bit = (flip >> 1) - (flip >> 3) - 2 * (flip >> 4)
    near = 768 + bit * 64 + (slot & 63)
    return jnp.where(slot < 768, slot, jnp.where(slot < 2816, near, slot - 1664))


def coef_index(slot, column):
    flip = lax.shift_right_arithmetic(slot - 768, 6) ^ column
    bit = (flip >> 1) - (flip >> 3) - 2 * (flip >> 4)
    near = jnp.where(bit < 4, 768 + bit * 32, 1024) + (slot & 31)
    far = 896 + jnp.where(slot < 2944, 0, 64) + (slot & 63)
    return jnp.where(slot < 768, slot, jnp.where(slot < 2816, near, far))


def physical(w, n, vn):
    rho, u, v, q, p = w
    kinetic = 0.5 * rho * (u * u + v * v + q * q)
    mass = rho * vn
    energy = (GAMMA / (GAMMA - 1.0) * p + kinetic) * vn
    return mass, mass * u + p * n[0], mass * v + p * n[1], mass * q + p * n[2], energy, kinetic


def entropy_fixed(eigen, sound):
    delta = 0.1 * sound
    magnitude = jnp.abs(eigen)
    return jnp.where(magnitude < delta, (eigen * eigen + delta * delta) / (2.0 * delta), magnitude)


def dot3(a, b):
    return a[0] * b[0] + a[1] * b[1] + a[2] * b[2]


def roe_flux(left, right, n):
    rho_l, u_l, p_l = left[0], left[1:4], left[4]
    rho_r, u_r, p_r = right[0], right[1:4], right[4]
    vn_l, vn_r = dot3(u_l, n), dot3(u_r, n)
    flux_l = physical(left, n, vn_l)
    flux_r = physical(right, n, vn_r)
    root_l, root_r = jnp.sqrt(rho_l), jnp.sqrt(rho_r)
    inverse = 1.0 / (root_l + root_r)
    part_l, part_r = root_l * inverse, root_r * inverse
    rho_a = root_l * root_r
    ratio = GAMMA / (GAMMA - 1.0)
    enth_l = (ratio * p_l + flux_l[5]) / rho_l
    enth_r = (ratio * p_r + flux_r[5]) / rho_r
    u_a = [part_l * a + part_r * b for a, b in zip(u_l, u_r)]
    enth_a = part_l * enth_l + part_r * enth_r
    half_speed = 0.5 * dot3(u_a, u_a)
    sound_sq = (GAMMA - 1.0) * (enth_a - half_speed)
    sound = jnp.sqrt(sound_sq)
    vn_a = dot3(u_a, n)
    d_rho, d_p = rho_r - rho_l, p_r - p_l
    d_u = [b - a for a, b in zip(u_l, u_r)]
    d_vn = dot3(d_u, n)
    per_sq = 1.0 / sound_sq
    slope = rho_a * sound * d_vn
    wave_1 = entropy_fixed(vn_a - sound, sound) * (d_p - slope) * (0.5 * per_sq)
    wave_5 = entropy_fixed(vn_a + sound, sound) * (d_p + slope) * (0.5 * per_sq)
    middle = entropy_fixed(vn_a, sound)
    wave_2 = middle * (d_rho - d_p * per_sq)
    shear = middle * rho_a
    both = wave_1 + wave_5
    total = both + wave_2
    across = sound * (wave_5 - wave_1)
    out = [flux_l[0] + flux_r[0] - total]
    tilt = across - shear * d_vn
    for i in range(3):
        out.append(flux_l[1 + i] + flux_r[1 + i] - (total * u_a[i] + tilt * n[i] + shear * d_u[i]))
    energy = (
        both * enth_a
        + across * vn_a
        + wave_2 * half_speed
        + shear * (dot3(u_a, d_u) - vn_a * d_vn)
    )
    out.append(flux_l[4] + flux_r[4] - energy)
    return out


def floored(w):
    return [jnp.maximum(w[0], FLOOR), w[1], w[2], w[3], jnp.maximum(w[4], FLOOR)]


def polynomials(coefs, side, tile, basis, part):
    low = iota(0) < 4
    place = (tile // 4) * 8 + tile % 4
    for point in range(2):
        terms = [coefs[r] * basis[side * 2 + point, r % 5, tile] for r in range(ROWS)]
        split = {r: (jnp.where(low, terms[r], 0.0), jnp.where(low, 0.0, terms[r])) for r in (2, 7)}
        sums = [
            terms[0] + terms[1] + split[2][0],
            split[2][1] + terms[3] + terms[4],
            terms[5] + terms[6] + split[7][0],
            split[7][1] + terms[8] + terms[9],
            terms[10] + terms[11] + jnp.where(low, terms[12], 0.0),
        ]
        for v in range(5):
            part[v, place + 4 * point] = sums[v]


def kernel(
    groups,
    state_h, pinv_h, sten_h, send_h, gids_h, fc_h, fg_h, fb_h,
    out_ref,
    st, pb, sn, sd, gi, fc, fg, fb,
    tbl, snd1, rcv1, snd2, rcv2, snd3, rcv3,
    nidx, pf, near, ctab, rgat, gtab, bas, bf32, inc, slots, geo,
    part, cen, left_w, wrow, wl,
    in_sem, s1, r1, s2, r2,
):
    g = lax.axis_index("group")
    d = lax.axis_index("dom")
    beside = [d + (1 << b) * (1 - 2 * ((d // (1 << b)) % 2)) for b in range(BITS)]
    has_low = g > 0
    has_high = g < groups - 1

    pairs = [(state_h, st), (send_h, sd), (gids_h, gi), (sten_h, sn), (pinv_h, pb), (fc_h, fc), (fb_h, fb), (fg_h, fg)]
    loads = [pltpu.make_async_copy(a, b, in_sem.at[i]) for i, (a, b) in enumerate(pairs)]
    for load in loads:
        load.start()

    barrier = pltpu.get_barrier_semaphore()
    for b in range(BITS):
        pl.semaphore_signal(barrier, inc=1, device_id=(g, beside[b]), device_id_type=MESH)

    @pl.when(has_low)
    def _():
        pl.semaphore_signal(barrier, inc=1, device_id=(g - 1, d), device_id_type=MESH)

    @pl.when(has_high)
    def _():
        pl.semaphore_signal(barrier, inc=1, device_id=(g + 1, d), device_id_type=MESH)

    def exchange(near_src, near_dst, far_src, far_dst, send, recv):
        copies = [
            pltpu.make_async_remote_copy(
                src_ref=near_src.at[b],
                dst_ref=near_dst.at[b],
                send_sem=send.at[b],
                recv_sem=recv.at[b],
                device_id=(g, beside[b]),
                device_id_type=MESH,
            )
            for b in range(BITS)
        ]
        up, down = [
            pltpu.make_async_remote_copy(
                src_ref=far_src(i),
                dst_ref=far_dst(i),
                send_sem=send.at[BITS + i],
                recv_sem=recv.at[BITS + i],
                device_id=(g + 1 - 2 * i, d),
                device_id_type=MESH,
            )
            for i in range(2)
        ]
        return copies, up, down

    def start(copies, up, down):
        for b in reversed(range(BITS)):
            copies[b].start()
        pl.when(has_high)(up.start)
        pl.when(has_low)(down.start)

    def received(copies, up, down):
        for copy in copies:
            copy.wait_recv()
        pl.when(has_low)(up.wait_recv)
        pl.when(has_high)(down.wait_recv)

    def sent(copies, up, down):
        for copy in copies:
            copy.wait_send()
        pl.when(has_high)(up.wait_send)
        pl.when(has_low)(down.wait_send)

    lane = iota(1)
    lower_half = lane < 64
    quarter = lane >> 5

    for load in loads[:3]:
        load.wait()
    for t in range(CT):
        tbl[t] = jnp.concatenate([st[:, t * 128 : (t + 1) * 128], jnp.zeros((3, 128), F32)], axis=0)
    own = [tbl[t] for t in range(CT)]
    near_ids = []
    for b in range(BITS):
        row = sd[pl.ds(beside[b], 1), :]
        near_ids.append(wide(jnp.concatenate([row, row], axis=1)))
    far_ids = [wide(gi[i : i + 1, :]) for i in range(2)]
    for i, ids in enumerate(near_ids + far_ids):
        snd1[i] = selected(own, ids & 127, ids >> 7, 0, None)

    first = exchange(
        snd1, rcv1, lambda i: snd1.at[BITS + i], lambda i: rcv1.at[BITS + i], s1, r1
    )
    second = exchange(snd2, rcv2, lambda i: snd3.at[i], lambda i: rcv3.at[i], s2, r2)
    pl.semaphore_wait(barrier, BITS + jnp.where(has_low, 1, 0) + jnp.where(has_high, 1, 0))
    start(*first)

    @pl.when(g == 0)
    def _():
        rcv1[BITS] = jnp.zeros((8, 128), F32)
        rcv3[0] = jnp.zeros((7, 8, 128), F32)

    @pl.when(g == groups - 1)
    def _():
        rcv1[BITS + 1] = jnp.zeros((8, 128), F32)
        rcv3[1] = jnp.zeros((7, 8, 128), F32)

    loads[3].wait()

    def own_neighbours(ct):
        for jt in range(JT):
            index = table_index(sn[jt * 8 : jt * 8 + 8, lanes_at(ct)], d)
            nidx[ct, jt] = index
            lanes, tile = index & 127, index >> 7
            for v in range(5):
                tiles = [wide(tbl[t, v : v + 1, :]) for t in range(CT)]
                near[ct, v, jt] = selected(tiles, lanes, tile, 0, None)

    loop(CT, own_neighbours)
    loads[4].wait()

    def widen(ct):
        for k in range(COEF):
            pf[ct, k] = pb[k, :, lanes_at(ct)].astype(F32)

    loop(CT, widen)

    received(*first)
    tbl[6] = jnp.where(lower_half, rcv1[0], rcv1[1])
    tbl[7] = jnp.where(lower_half, rcv1[2], rcv1[3])
    tbl[8] = rcv1[4]
    tbl[9] = rcv1[5]
    tbl[10] = rcv1[6]

    def coefficients(ct):
        diffs = [[None] * JT for _ in range(5)]
        for jt in range(JT):
            index = nidx[ct, jt]
            lanes, tile = index & 127, index >> 7
            for v in range(5):
                tiles = [wide(tbl[t, v : v + 1, :]) for t in range(CT, 11)]
                value = selected(tiles, lanes, tile, CT, near[ct, v, jt])
                diff = value - wide(tbl[ct, v : v + 1, :])
                diffs[v][jt] = diff.astype(BF16).astype(F32)
        for r in range(ROWS):
            parts = []
            for s in range(8):
                v, k = divmod(8 * r + s, COEF)
                if v > 4:
                    parts.append(jnp.zeros((8, 128), F32))
                    continue
                acc = None
                for jt in range(JT):
                    term = pf[ct, k, jt * 8 : jt * 8 + 8, :] * diffs[v][jt]
                    acc = term if acc is None else acc + term
                parts.append(acc)
            ctab[r, ct] = row_sums(parts)

    loop(CT, coefficients)

    spread = [lane_gather(ids, lane & 31) for ids in near_ids]
    mixed = spread[0]
    for q in range(1, 4):
        mixed = jnp.where(quarter == q, spread[q], mixed)
    turned = [mixed] + [pltpu.roll(mixed, 32 * a, 1) for a in range(1, 4)]
    ends = jnp.where(lower_half, far_ids[0], pltpu.roll(far_ids[1], 64, 1))
    ends = [ends, pltpu.roll(ends, 64, 1)]

    def picked(r, ids):
        return selected([ctab[r, t] for t in range(CT)], ids & 127, ids >> 7, 0, None)

    for m in range(4):
        rows = range(4 * m, min(4 * m + 4, ROWS))
        got = [picked(r, turned[r % 4]) for r in rows]
        last = [picked(r, spread[4]) for r in rows]
        if len(got) == 1:
            for b in range(4):
                snd2[b, m] = got[0]
            snd2[4, m] = last[0]
            continue
        for b in range(4):
            mix = got[-b % 4]
            for q in range(1, 4):
                mix = jnp.where(quarter == q, got[(q - b) % 4], mix)
            snd2[b, m] = mix
        mix = last[0]
        for q in range(1, 4):
            mix = jnp.where(quarter == q, last[q], mix)
        snd2[4, m] = mix
    for m in range(7):
        rows = range(2 * m, min(2 * m + 2, ROWS))
        got = [picked(r, ends[r % 2]) for r in rows]
        snd3[0, m] = jnp.where(lower_half, got[0], got[-1])
        snd3[1, m] = jnp.where(lower_half, got[-1], got[0])
    start(*second)

    for load in loads[5:]:
        load.wait()

    def unpack_basis(ft):
        at = lanes_at(ft)
        bf32[ft] = fb[:, at].astype(F32)
        for i in range(4):
            base = 20 * i
            bas[i, 0, ft] = bf32[ft, base : base + 8, :]
            bas[i, 1, ft] = bf32[ft, base + 8 : base + 16, :]
            bas[i, 2, ft] = jnp.concatenate(
                [bf32[ft, base + 16 : base + 20, :], bf32[ft, base : base + 4, :]], axis=0
            )
            bas[i, 3, ft] = bf32[ft, base + 4 : base + 12, :]
            bas[i, 4, ft] = bf32[ft, base + 12 : base + 20, :]

    loop(FT, unpack_basis)

    def left_side(ft):
        slot = wide(fc[0:1, lanes_at(ft)])
        lanes, tile = slot & 127, slot >> 7
        coefs = [
            selected([ctab[r, t] for t in range(CT)], lanes, tile, 0, None) for r in range(ROWS)
        ]
        polynomials(coefs, 0, ft, bas, part)

    loop(FT, left_side)

    def right_own(ft):
        slot = wide(fc[1:2, lanes_at(ft)])
        lanes, tile = slot & 127, slot >> 7
        for r in range(ROWS):
            rgat[ft, r] = selected([ctab[r, t] for t in range(CT)], lanes, tile, 0, None)

    loop(FT, right_own)

    for ft in range(FT):
        at = slice(ft * 128, ft * 128 + 128)
        for i in range(2):
            row = i * 4 + ft % 4
            for e in range(2):
                slots[e, ft // 4, row : row + 1, :] = fc[e : e + 1, at]
            for e in range(4):
                geo[e, ft // 4, row : row + 1, :] = fg[e : e + 1, at]

    def centres(u):
        slot = slots[0, u]
        for v in range(5):
            tiles = [wide(tbl[t, v : v + 1, :]) for t in range(CT)]
            cen[0, v, u] = selected(tiles, slot & 127, slot >> 7, 0, None)
        index = table_index(slots[1, u], d)
        for v in range(5):
            tiles = [wide(tbl[t, v : v + 1, :]) for t in range(11)]
            cen[1, v, u] = selected(tiles, index & 127, index >> 7, 0, None)
        for v in range(5):
            left_w[v, u] = cen[0, v, u] + row_sums([part[v, u * 8 + s] for s in range(8)])

    loop(UT, centres)

    def incidence(ft):
        at = lanes_at(ft)
        cell = lax.broadcasted_iota(I32, (CELLS, 128), 0)
        sign = jnp.where(
            cell == fc[0:1, at], 1.0, jnp.where(cell == fc[1:2, at], -1.0, 0.0)
        )
        inc[:, at] = sign.astype(BF16)

    loop(FT, incidence)

    received(*second)

    for r in range(ROWS):
        m, a = divmod(r, 4)
        mix = rcv2[-a % 4, m]
        for q in range(1, 4):
            mix = jnp.where(quarter == q, rcv2[(q - a) % 4, m], mix)
        gtab[r, 0] = mix
        gtab[r, 1] = jnp.where(lower_half, rcv3[r % 2, r // 2], rcv3[1 - r % 2, r // 2])
        gtab[r, 2] = rcv2[4, m]

    def right_side(ft):
        index = coef_index(wide(fc[1:2, lanes_at(ft)]), d)
        tile = index >> 7
        lanes = [(index + 32 * a) & 127 for a in range(4)]
        coefs = []
        for r in range(ROWS):
            acc = rgat[ft, r]
            for i, a in enumerate((r % 4, 2 * (r % 2), r % 4)):
                acc = selected([gtab[r, i]], lanes[a], tile, CT + i, acc)
            coefs.append(acc)
        polynomials(coefs, 1, ft, bas, part)

    loop(FT, right_side)

    wrow[...] = jnp.zeros((FT, 8, 128), F32)

    def fluxes(u):
        left = floored([left_w[v, u] for v in range(5)])
        right = [cen[1, v, u] + row_sums([part[v, u * 8 + s] for s in range(8)]) for v in range(5)]
        flux = roe_flux(left, floored(right), [geo[i, u] for i in range(3)])
        scale = 0.25 * geo[3, u]
        for v in range(5):
            weighted = scale * flux[v]
            weighted = weighted + pltpu.roll(weighted, 4, 0)
            for i in range(4):
                wrow[u * 4 + i, v : v + 1, :] = weighted[i : i + 1, :]

    loop(UT, fluxes)

    def split(ft):
        whole = wrow[ft]
        high = whole.astype(BF16).astype(F32)
        wl[:, lanes_at(ft)] = jnp.concatenate([high, whole - high], axis=0).astype(BF16)

    loop(FT, split)
    summed = lax.dot_general(
        wl[...], inc[...], (((1,), (1,)), ((), ())), preferred_element_type=F32
    )
    out_ref[...] = summed[0:5] + summed[8:13]
    sent(*first)
    sent(*second)


def per_device(groups, *args):
    any_spec = pl.BlockSpec(memory_space=pl.ANY)
    vmem = pltpu.VMEM
    tile = (8, 128)
    scratch = [
        vmem((5, CELLS), F32),
        vmem((COEF, STEN, CELLS), BF16),
        vmem((STEN, CELLS), I32),
        vmem(args[3].shape, I32),
        vmem((2, 128), I32),
        vmem((2, FACES), I32),
        vmem((4, FACES), F32),
        vmem((80, FACES), BF16),
        vmem((11,) + tile, F32),
        vmem((7,) + tile, F32),
        vmem((7,) + tile, F32),
        vmem((BITS, 4) + tile, F32),
        vmem((BITS, 4) + tile, F32),
        vmem((2, 7) + tile, F32),
        vmem((2, 7) + tile, F32),
        vmem((CT, JT) + tile, I32),
        vmem((CT, COEF, STEN, 128), F32),
        vmem((CT, 5, JT) + tile, F32),
        vmem((ROWS, CT) + tile, F32),
        vmem((FT, ROWS) + tile, F32),
        vmem((ROWS, 3) + tile, F32),
        vmem((4, 5, FT) + tile, F32),
        vmem((FT, 80, 128), F32),
        vmem((CELLS, FACES), BF16),
        vmem((2, UT) + tile, I32),
        vmem((4, UT) + tile, F32),
        vmem((5, 2 * FT) + tile, F32),
        vmem((2, 5, UT) + tile, F32),
        vmem((5, UT) + tile, F32),
        vmem((FT,) + tile, F32),
        vmem((16, FACES), BF16),
        pltpu.SemaphoreType.DMA((8,)),
        pltpu.SemaphoreType.DMA((7,)),
        pltpu.SemaphoreType.DMA((7,)),
        pltpu.SemaphoreType.DMA((7,)),
        pltpu.SemaphoreType.DMA((7,)),
    ]
    return pl.pallas_call(
        functools.partial(kernel, groups),
        out_shape=jax.ShapeDtypeStruct((5, CELLS), F32),
        in_specs=[any_spec] * 8,
        out_specs=pl.BlockSpec(memory_space=pltpu.VMEM),
        scratch_shapes=scratch,
        compiler_params=pltpu.CompilerParams(
            collective_id=0, has_side_effects=True, vmem_limit_bytes=56 * 1024 * 1024
        ),
    )(*args)


def solution(mesh):
    both = ("group", "dom")
    in_specs = (
        P(None, both),
        P(None, None, both),
        P(None, both),
        P(both, None),
        P(both, None),
        P(None, both),
        P(None, both),
        P(None, both),
    )
    return jax.shard_map(
        functools.partial(per_device, mesh.shape["group"]),
        mesh=mesh,
        in_specs=in_specs,
        out_specs=P(None, both),
        check_vma=False,
    )
```

```python
import functools

import jax
import jax.numpy as jnp
from jax import lax
from jax.experimental import pallas as pl
from jax.experimental.pallas import tpu as pltpu
from jax.sharding import PartitionSpec as P

GAMMA = 1.4
FLOOR = 0.2
MESH = pl.DeviceIdType.MESH
F32 = jnp.float32
BF16 = jnp.bfloat16
I32 = jnp.int32

CELLS = 768
FACES = 1536
CT = CELLS // 128
FT = FACES // 128
COEF = 20
STEN = 40
JT = STEN // 8
ROWS = 13
BITS = 5
ORDER = (4, 1, 3, 0, 2)
UT = FT // 4


def loop(count, body):
    def step(i, carry):
        body(i)
        return carry

    lax.fori_loop(0, count, step, 0)


def lanes_at(tile):
    return pl.ds(pl.multiple_of(tile * 128, 128), 128)


def lane_gather(values, lanes):
    return jnp.take_along_axis(values, lanes, axis=1, mode="promise_in_bounds")


def wide(row):
    return jnp.broadcast_to(row, (8, 128))


def iota(axis):
    return lax.broadcasted_iota(I32, (8, 128), axis)


def row_sums(ref):
    x = [ref[pl.ds(j, 8, stride=8), :] for j in range(8)]
    return ((x[0] + x[1]) + (x[2] + x[3])) + ((x[4] + x[5]) + (x[6] + x[7]))


def selected(tiles, lanes, tile, start, acc):
    for i, values in enumerate(tiles):
        got = lane_gather(values, lanes)
        acc = got if acc is None else jnp.where(tile == start + i, got, acc)
    return acc


def table_index(slot, column):
    flip = lax.shift_right_arithmetic(slot - 768, 6) ^ column
    bit = (flip >> 1) - (flip >> 3) - 2 * (flip >> 4)
    near = 768 + bit * 64 + (slot & 63)
    return jnp.where(slot < 768, slot, jnp.where(slot < 2816, near, slot - 1664))


def coef_index(slot, column):
    flip = lax.shift_right_arithmetic(slot - 768, 6) ^ column
    bit = (flip >> 1) - (flip >> 3) - 2 * (flip >> 4)
    near = jnp.where(bit < 4, 768 + bit * 32, 1024) + (slot & 31)
    far = 896 + jnp.where(slot < 2944, 0, 64) + (slot & 63)
    return jnp.where(slot < 768, slot, jnp.where(slot < 2816, near, far))


def physical(w, n, vn):
    rho, u, v, q, p = w
    kinetic = 0.5 * rho * (u * u + v * v + q * q)
    mass = rho * vn
    energy = (GAMMA / (GAMMA - 1.0) * p + kinetic) * vn
    return mass, mass * u + p * n[0], mass * v + p * n[1], mass * q + p * n[2], energy, kinetic


def entropy_fixed(eigen, sound):
    delta = 0.1 * sound
    magnitude = jnp.abs(eigen)
    return jnp.where(magnitude < delta, (eigen * eigen + delta * delta) / (2.0 * delta), magnitude)


def dot3(a, b):
    return a[0] * b[0] + a[1] * b[1] + a[2] * b[2]


def roe_flux(left, right, n):
    rho_l, u_l, p_l = left[0], left[1:4], left[4]
    rho_r, u_r, p_r = right[0], right[1:4], right[4]
    vn_l, vn_r = dot3(u_l, n), dot3(u_r, n)
    flux_l = physical(left, n, vn_l)
    flux_r = physical(right, n, vn_r)
    root_l, root_r = jnp.sqrt(rho_l), jnp.sqrt(rho_r)
    inverse = 1.0 / (root_l + root_r)
    part_l, part_r = root_l * inverse, root_r * inverse
    rho_a = root_l * root_r
    ratio = GAMMA / (GAMMA - 1.0)
    enth_l = (ratio * p_l + flux_l[5]) / rho_l
    enth_r = (ratio * p_r + flux_r[5]) / rho_r
    u_a = [part_l * a + part_r * b for a, b in zip(u_l, u_r)]
    enth_a = part_l * enth_l + part_r * enth_r
    half_speed = 0.5 * dot3(u_a, u_a)
    sound_sq = (GAMMA - 1.0) * (enth_a - half_speed)
    sound = jnp.sqrt(sound_sq)
    vn_a = dot3(u_a, n)
    d_rho, d_p = rho_r - rho_l, p_r - p_l
    d_u = [b - a for a, b in zip(u_l, u_r)]
    d_vn = dot3(d_u, n)
    per_sq = 1.0 / sound_sq
    slope = rho_a * sound * d_vn
    wave_1 = entropy_fixed(vn_a - sound, sound) * (d_p - slope) * (0.5 * per_sq)
    wave_5 = entropy_fixed(vn_a + sound, sound) * (d_p + slope) * (0.5 * per_sq)
    middle = entropy_fixed(vn_a, sound)
    wave_2 = middle * (d_rho - d_p * per_sq)
    shear = middle * rho_a
    both = wave_1 + wave_5
    total = both + wave_2
    across = sound * (wave_5 - wave_1)
    out = [flux_l[0] + flux_r[0] - total]
    tilt = across - shear * d_vn
    for i in range(3):
        out.append(flux_l[1 + i] + flux_r[1 + i] - (total * u_a[i] + tilt * n[i] + shear * d_u[i]))
    energy = (
        both * enth_a
        + across * vn_a
        + wave_2 * half_speed
        + shear * (dot3(u_a, d_u) - vn_a * d_vn)
    )
    out.append(flux_l[4] + flux_r[4] - energy)
    return out


def floored(w):
    return [jnp.maximum(w[0], FLOOR), w[1], w[2], w[3], jnp.maximum(w[4], FLOOR)]


def polynomials(coefs, side, u, f, basis, part):
    low = iota(0) < 4
    for point in range(2):
        terms = [coefs[r] * basis[side * 2 + point, r % 5, u * 4 + f] for r in range(ROWS)]
        split = {r: (jnp.where(low, terms[r], 0.0), jnp.where(low, 0.0, terms[r])) for r in (2, 7)}
        sums = [
            (terms[0] + terms[1]) + split[2][0],
            (terms[3] + terms[4]) + split[2][1],
            (terms[5] + terms[6]) + split[7][0],
            (terms[8] + terms[9]) + split[7][1],
            (terms[10] + terms[11]) + jnp.where(low, terms[12], 0.0),
        ]
        place = (point * 4 + f) * 8
        for v in range(5):
            part[v, u, place : place + 8, :] = sums[v]


def kernel(
    groups,
    state_h, pinv_h, sten_h, send_h, gids_h, fc_h, fg_h, fb_h,
    out_ref,
    st, pb, sn, sd, gi, fc, fg, fb,
    tbl, snd1, rcv1, snd2, rcv2, snd3, rcv3,
    nidx, ridx, pf, near, ctab, rgat, gtab, bas, bf32, hot, slots, geo,
    part, terms, cen, left_w, turn, wl,
    in_sem, s1, r1, s2, r2,
):
    g = lax.axis_index("group")
    d = lax.axis_index("dom")
    beside = [d + (1 << b) * (1 - 2 * ((d // (1 << b)) % 2)) for b in range(BITS)]
    has_low = g > 0
    has_high = g < groups - 1

    barrier = pltpu.get_barrier_semaphore()
    for b in ORDER:
        pl.semaphore_signal(barrier, inc=1, device_id=(g, beside[b]), device_id_type=MESH)

    @pl.when(has_low)
    def _():
        pl.semaphore_signal(barrier, inc=1, device_id=(g - 1, d), device_id_type=MESH)

    @pl.when(has_high)
    def _():
        pl.semaphore_signal(barrier, inc=1, device_id=(g + 1, d), device_id_type=MESH)

    pairs = [(state_h, st), (send_h, sd), (gids_h, gi), (sten_h, sn), (pinv_h, pb), (fc_h, fc), (fb_h, fb), (fg_h, fg)]
    loads = [pltpu.make_async_copy(a, b, in_sem.at[i]) for i, (a, b) in enumerate(pairs)]
    for load in loads:
        load.start()

    def exchange(near_src, near_dst, far_src, far_dst, send, recv):
        copies = [
            pltpu.make_async_remote_copy(
                src_ref=near_src.at[b],
                dst_ref=near_dst.at[b],
                send_sem=send.at[b],
                recv_sem=recv.at[b],
                device_id=(g, beside[b]),
                device_id_type=MESH,
            )
            for b in range(BITS)
        ]
        up, down = [
            pltpu.make_async_remote_copy(
                src_ref=far_src(i),
                dst_ref=far_dst(i),
                send_sem=send.at[BITS + i],
                recv_sem=recv.at[BITS + i],
                device_id=(g + 1 - 2 * i, d),
                device_id_type=MESH,
            )
            for i in range(2)
        ]
        return copies, up, down

    def start_far(copies, up, down):
        pl.when(has_high)(up.start)
        pl.when(has_low)(down.start)

    def received(copies, up, down):
        for b in reversed(ORDER[1:]):
            copies[b].wait_recv()
        pl.when(has_low)(up.wait_recv)
        pl.when(has_high)(down.wait_recv)

    def sent(copies, up, down):
        for copy in copies:
            copy.wait_send()
        pl.when(has_high)(up.wait_send)
        pl.when(has_low)(down.wait_send)

    lane = iota(1)
    lower_half = lane < 64
    quarter = lane >> 5

    for load in loads[:3]:
        load.wait()
    for t in range(CT):
        tbl[t] = jnp.concatenate([st[:, t * 128 : (t + 1) * 128], jnp.zeros((3, 128), F32)], axis=0)
    own = [tbl[t] for t in range(CT)]
    near_ids = []
    for b in range(BITS):
        row = sd[pl.ds(beside[b], 1), :]
        near_ids.append(wide(jnp.concatenate([row, row], axis=1)))
    far_ids = [wide(gi[i : i + 1, :]) for i in range(2)]
    for i, ids in enumerate(near_ids + far_ids):
        snd1[i] = selected(own, ids & 127, ids >> 7, 0, None)

    first = exchange(
        snd1, rcv1, lambda i: snd1.at[BITS + i], lambda i: rcv1.at[BITS + i], s1, r1
    )
    second = exchange(snd2, rcv2, lambda i: snd3.at[i], lambda i: rcv3.at[i], s2, r2)
    pl.semaphore_wait(barrier, BITS + jnp.where(has_low, 1, 0) + jnp.where(has_high, 1, 0))
    for b in ORDER:
        first[0][b].start()
    start_far(*first)

    @pl.when(g == 0)
    def _():
        rcv1[BITS] = jnp.zeros((8, 128), F32)
        rcv3[0] = jnp.zeros((7, 8, 128), F32)

    @pl.when(g == groups - 1)
    def _():
        rcv1[BITS + 1] = jnp.zeros((8, 128), F32)
        rcv3[1] = jnp.zeros((7, 8, 128), F32)

    loads[3].wait()

    def own_neighbours(ct):
        for jt in range(JT):
            index = table_index(sn[jt * 8 : jt * 8 + 8, lanes_at(ct)], d)
            nidx[ct, jt] = index
            lanes, tile = index & 127, index >> 7
            for v in range(5):
                tiles = [wide(tbl[t, v : v + 1, :]) for t in range(CT)]
                near[ct, v, jt] = selected(tiles, lanes, tile, 0, None)

    loop(CT, own_neighbours)
    for load in loads[4:]:
        load.wait()

    def widen(ct):
        for k in range(COEF):
            pf[ct, k] = pb[k, :, lanes_at(ct)].astype(F32)

    loop(CT, widen)

    def unpack_basis(ft):
        at = lanes_at(ft)
        bf32[ft] = fb[:, at].astype(F32)
        for i in range(4):
            base = 20 * i
            bas[i, 0, ft] = bf32[ft, base : base + 8, :]
            bas[i, 1, ft] = bf32[ft, base + 8 : base + 16, :]
            bas[i, 2, ft] = jnp.concatenate(
                [bf32[ft, base + 16 : base + 20, :], bf32[ft, base : base + 4, :]], axis=0
            )
            bas[i, 3, ft] = bf32[ft, base + 4 : base + 12, :]
            bas[i, 4, ft] = bf32[ft, base + 12 : base + 20, :]
        cell = lax.broadcasted_iota(I32, (128, 128), 0)
        for e in range(2):
            same = cell == (fc[e : e + 1, at] & 127)
            hot[e * 128 : e * 128 + 128, at] = jnp.where(same, 1.0, 0.0).astype(BF16)
        ridx[ft] = coef_index(wide(fc[1:2, at]), d)

    loop(FT, unpack_basis)

    for ft in range(FT):
        at = slice(ft * 128, ft * 128 + 128)
        for i in range(2):
            row = i * 4 + ft % 4
            for e in range(2):
                slots[e, ft // 4, row : row + 1, :] = fc[e : e + 1, at]
            for e in range(4):
                geo[e, ft // 4, row : row + 1, :] = fg[e : e + 1, at]

    received(*first)
    tbl[6] = jnp.where(lower_half, rcv1[0], rcv1[1])
    tbl[7] = jnp.where(lower_half, rcv1[2], rcv1[3])
    tbl[9] = rcv1[5]
    tbl[10] = rcv1[6]

    def other_neighbours(ct):
        for jt in range(JT):
            index = nidx[ct, jt]
            lanes, tile = index & 127, index >> 7
            for v in range(5):
                acc = near[ct, v, jt]
                for t in (6, 7, 9, 10):
                    acc = selected([wide(tbl[t, v : v + 1, :])], lanes, tile, t, acc)
                near[ct, v, jt] = acc

    for i in range(6): other_neighbours(i)

    first[0][4].wait_recv()
    tbl[8] = rcv1[4]

    def coefficients(pair):
        for i in range(6):
            ct = i
            diffs = [[None] * JT for _ in range(5)]
            for jt in range(JT):
                index = nidx[ct, jt]
                lanes, tile = index & 127, index >> 7
                for v in range(5):
                    value = selected([wide(tbl[8, v : v + 1, :])], lanes, tile, 8, near[ct, v, jt])
                    diff = value - wide(tbl[ct, v : v + 1, :])
                    diffs[v][jt] = diff.astype(BF16).astype(F32)
            for r in range(ROWS):
                for s in range(8):
                    v, k = divmod(8 * r + s, COEF)
                    if v > 4:
                        continue
                    x = [pf[ct, k, jt * 8 : jt * 8 + 8, :] * diffs[v][jt] for jt in range(JT)]
                    terms[i, r, s * 8 : s * 8 + 8, :] = ((x[0] + x[1]) + (x[2] + x[3])) + x[4]
            for r in range(ROWS):
                ctab[r, ct] = row_sums(terms.at[i, r])

    terms[:, ROWS - 1, 32:64, :] = jnp.zeros((6, 32, 128), F32)
    coefficients(0)

    spread = [lane_gather(ids, lane & 31) for ids in near_ids]
    mixed = spread[0]
    for q in range(1, 4):
        mixed = jnp.where(quarter == q, spread[q], mixed)
    turned = [mixed] + [pltpu.roll(mixed, 32 * a, 1) for a in range(1, 4)]
    ends = jnp.where(lower_half, far_ids[0], pltpu.roll(far_ids[1], 64, 1))
    ends = [ends, pltpu.roll(ends, 64, 1)]

    def picked(r, ids):
        return selected([ctab[r, t] for t in range(CT)], ids & 127, ids >> 7, 0, None)

    groups_of = [range(4 * m, min(4 * m + 4, ROWS)) for m in range(4)]
    for m, rows in enumerate(groups_of):
        got = [picked(r, spread[4]) for r in rows]
        mix = got[0]
        for q in range(1, len(got)):
            mix = jnp.where(quarter == q, got[q], mix)
        snd2[4, m] = mix
    second[0][4].start()
    for m, rows in enumerate(groups_of):
        got = [picked(r, turned[r % 4]) for r in rows]
        for b in range(4):
            mix = got[-b % len(got)]
            for q in range(1, len(got)):
                mix = jnp.where(quarter == q, got[(q - b) % 4], mix)
            snd2[b, m] = mix
    for b in ORDER[1:]:
        second[0][b].start()
    for m in range(7):
        rows = range(2 * m, min(2 * m + 2, ROWS))
        got = [picked(r, ends[r % 2]) for r in rows]
        snd3[0, m] = jnp.where(lower_half, got[0], got[-1])
        snd3[1, m] = jnp.where(lower_half, got[-1], got[0])
    start_far(*second)

    def left_side(u):
        for f in range(4):
            slot = wide(fc[0:1, lanes_at(u * 4 + f)])
            lanes, tile = slot & 127, slot >> 7
            coefs = [
                selected([ctab[r, t] for t in range(CT)], lanes, tile, 0, None)
                for r in range(ROWS)
            ]
            polynomials(coefs, 0, u, f, bas, part)

    loop(UT, left_side)

    def right_own(u):
        for f in range(4):
            index = ridx[u * 4 + f]
            lanes, tile = index & 127, index >> 7
            for r in range(ROWS):
                own_part = selected([ctab[r, t] for t in range(CT)], lanes, tile, 0, None)
                rgat[u * 4 + f, r] = own_part

    loop(UT, right_own)

    def centres(u):
        slot = slots[0, u]
        for v in range(5):
            tiles = [wide(tbl[t, v : v + 1, :]) for t in range(CT)]
            centre = selected(tiles, slot & 127, slot >> 7, 0, None)
            left_w[v, u] = centre + row_sums(part.at[v, u])
        index = table_index(slots[1, u], d)
        for v in range(5):
            tiles = [wide(tbl[t, v : v + 1, :]) for t in range(11)]
            cen[v, u] = selected(tiles, index & 127, index >> 7, 0, None)

    loop(UT, centres)

    received(*second)

    for r in range(ROWS):
        m, a = divmod(r, 4)
        mix = rcv2[-a % 4, m]
        for q in range(1, 4):
            mix = jnp.where(quarter == q, rcv2[(q - a) % 4, m], mix)
        gtab[r, 0] = mix
        gtab[r, 1] = jnp.where(lower_half, rcv3[r % 2, r // 2], rcv3[1 - r % 2, r // 2])

    def right_near(u):
        for f in range(4):
            index = ridx[u * 4 + f]
            tile = index >> 7
            lanes = [(index + 32 * a) & 127 for a in range(4)]
            for r in range(ROWS):
                acc = rgat[u * 4 + f, r]
                acc = selected([gtab[r, 0]], lanes[r % 4], tile, 6, acc)
                rgat[u * 4 + f, r] = selected([gtab[r, 1]], lanes[2 * (r % 2)], tile, 7, acc)

    for u in range(UT): right_near(u)
    turn[...] = jnp.zeros((UT, 64, 128), F32)
    second[0][4].wait_recv()

    total = None
    for u in range(UT):
        for f in range(4):
            index = ridx[u * 4 + f]
            tile = index >> 7
            lanes = [(index + 32 * a) & 127 for a in range(4)]
            coefs = [
                selected([rcv2[4, r // 4]], lanes[r % 4], tile, 8, rgat[u * 4 + f, r])
                for r in range(ROWS)
            ]
            polynomials(coefs, 1, u, f, bas, part)
        left = floored([left_w[v, u] for v in range(5)])
        right = floored([cen[v, u] + row_sums(part.at[v, u]) for v in range(5)])
        flux = roe_flux(left, right, [geo[i, u] for i in range(3)])
        scale = 0.25 * geo[3, u]
        for v in range(5):
            weighted = scale * flux[v]
            turn[u, v * 8 : v * 8 + 8, :] = weighted + pltpu.roll(weighted, 4, 0)
        for f in range(4):
            at = slice((u * 4 + f) * 128, (u * 4 + f + 1) * 128)
            whole = turn[u, pl.ds(f, 8, stride=8), :]
            high = whole.astype(BF16).astype(F32)
            rest = whole - high
            for e in range(2):
                tile = wide(fc[e : e + 1, at]) >> 7
                for t in range(CT):
                    mask = tile == t
                    rows = [jnp.where(mask, high, 0.0), jnp.where(mask, rest, 0.0)]
                    place = (e * CT + t) * 16
                    wl[place : place + 16, at] = jnp.concatenate(rows, axis=0).astype(BF16)
        at = slice(u * 512, u * 512 + 512)
        summed = lax.dot_general(
            wl[:, at], hot[:, at], (((1,), (1,)), ((), ())), preferred_element_type=F32
        )
        total = summed if total is None else total + summed
    for t in range(CT):
        gained = total[t * 16 : t * 16 + 16, 0:128]
        lost = total[(CT + t) * 16 : (CT + t) * 16 + 16, 128:256]
        change = gained - lost
        out_ref[:, t * 128 : t * 128 + 128] = (change[0:8] + change[8:16])[0:5]
    sent(*first)
    sent(*second)


def per_device(groups, *args):
    any_spec = pl.BlockSpec(memory_space=pl.ANY)
    vmem = pltpu.VMEM
    tile = (8, 128)
    scratch = [
        vmem((5, CELLS), F32),
        vmem((COEF, STEN, CELLS), BF16),
        vmem((STEN, CELLS), I32),
        vmem(args[3].shape, I32),
        vmem((2, 128), I32),
        vmem((2, FACES), I32),
        vmem((4, FACES), F32),
        vmem((80, FACES), BF16),
        vmem((11,) + tile, F32),
        vmem((7,) + tile, F32),
        vmem((7,) + tile, F32),
        vmem((BITS, 4) + tile, F32),
        vmem((BITS, 4) + tile, F32),
        vmem((2, 7) + tile, F32),
        vmem((2, 7) + tile, F32),
        vmem((CT, JT) + tile, I32),
        vmem((FT,) + tile, I32),
        vmem((CT, COEF, STEN, 128), F32),
        vmem((CT, 5, JT) + tile, F32),
        vmem((ROWS, CT) + tile, F32),
        vmem((FT, ROWS) + tile, F32),
        vmem((ROWS, 2) + tile, F32),
        vmem((4, 5, FT) + tile, F32),
        vmem((FT, 80, 128), F32),
        vmem((256, FACES), BF16),
        vmem((2, UT) + tile, I32),
        vmem((4, UT) + tile, F32),
        vmem((5, UT, 64, 128), F32),
        vmem((6, ROWS, 64, 128), F32),
        vmem((5, UT) + tile, F32),
        vmem((5, UT) + tile, F32),
        vmem((UT, 64, 128), F32),
        vmem((192, FACES), BF16),
        pltpu.SemaphoreType.DMA((8,)),
        pltpu.SemaphoreType.DMA((7,)),
        pltpu.SemaphoreType.DMA((7,)),
        pltpu.SemaphoreType.DMA((7,)),
        pltpu.SemaphoreType.DMA((7,)),
    ]
    return pl.pallas_call(
        functools.partial(kernel, groups),
        out_shape=pltpu.VMEM((5, CELLS), F32),
        in_specs=[any_spec] * 8,
        out_specs=pl.BlockSpec(memory_space=pltpu.VMEM),
        scratch_shapes=scratch,
        compiler_params=pltpu.CompilerParams(
            collective_id=0, has_side_effects=True, vmem_limit_bytes=56 * 1024 * 1024
        ),
    )(*args)


def solution(mesh):
    both = ("group", "dom")
    in_specs = (
        P(None, both),
        P(None, None, both),
        P(None, both),
        P(both, None),
        P(both, None),
        P(None, both),
        P(None, both),
        P(None, both),
    )
    return jax.shard_map(
        functools.partial(per_device, mesh.shape["group"]),
        mesh=mesh,
        in_specs=in_specs,
        out_specs=P(None, both),
        check_vma=False,
    )
```

```python
import functools

import jax
import jax.numpy as jnp
from jax import lax
from jax.experimental import pallas as pl
from jax.experimental.pallas import tpu as pltpu
from jax.sharding import PartitionSpec as P

GAMMA = 1.4
FLOOR = 0.2
MESH = pl.DeviceIdType.MESH
F32 = jnp.float32
BF16 = jnp.bfloat16
I32 = jnp.int32

CELLS = 768
FACES = 1536
CT = CELLS // 128
FT = FACES // 128
COEF = 20
STEN = 40
JT = STEN // 8
ROWS = 13
BITS = 5
ORDER = (4, 1, 3, 0, 2)
UT = FT // 4

EARLY = ()
LATE = (0, 1, 2, 3, 4, "ends")
EARLY_COEFS = (0, 1, 2, 3, 4)
LATE_COEFS = ("ends",)
TABLE_TILES = {0: (6, 7), 4: (8,), "ends": (9, 10)}
GHOST_TILES = {0: (0,), 4: (2,), "ends": (1,)}


def tiles_of(kinds, tiles):
    return [t for kind, of in tiles.items() if kind in kinds for t in of]


def loop(count, body):
    def step(i, carry):
        body(i)
        return carry

    lax.fori_loop(0, count, step, 0)


def lanes_at(tile):
    return pl.ds(pl.multiple_of(tile * 128, 128), 128)


def lane_gather(values, lanes):
    return jnp.take_along_axis(values, lanes, axis=1, mode="promise_in_bounds")


def wide(row):
    return jnp.broadcast_to(row, (8, 128))


def iota(axis):
    return lax.broadcasted_iota(I32, (8, 128), axis)


def row_sums(ref):
    x = [ref[pl.ds(j, 8, stride=8), :] for j in range(8)]
    return ((x[0] + x[1]) + (x[2] + x[3])) + ((x[4] + x[5]) + (x[6] + x[7]))


def selected(tiles, lanes, tile, start, acc):
    for i, values in enumerate(tiles):
        got = lane_gather(values, lanes)
        acc = got if acc is None else jnp.where(tile == start + i, got, acc)
    return acc


def table_index(slot, column):
    flip = lax.shift_right_arithmetic(slot - 768, 6) ^ column
    bit = (flip >> 1) - (flip >> 3) - 2 * (flip >> 4)
    near = 768 + bit * 64 + (slot & 63)
    return jnp.where(slot < 768, slot, jnp.where(slot < 2816, near, slot - 1664))


def coef_index(slot, column):
    flip = lax.shift_right_arithmetic(slot - 768, 6) ^ column
    bit = (flip >> 1) - (flip >> 3) - 2 * (flip >> 4)
    near = jnp.where(bit < 4, 768 + bit * 32, 1024) + (slot & 31)
    far = 896 + jnp.where(slot < 2944, 0, 64) + (slot & 63)
    return jnp.where(slot < 768, slot, jnp.where(slot < 2816, near, far))


def physical(w, n, vn):
    rho, u, v, q, p = w
    kinetic = 0.5 * rho * (u * u + v * v + q * q)
    mass = rho * vn
    energy = (GAMMA / (GAMMA - 1.0) * p + kinetic) * vn
    return mass, mass * u + p * n[0], mass * v + p * n[1], mass * q + p * n[2], energy, kinetic


def entropy_fixed(eigen, sound):
    delta = 0.1 * sound
    magnitude = jnp.abs(eigen)
    return jnp.where(magnitude < delta, (eigen * eigen + delta * delta) / (2.0 * delta), magnitude)


def dot3(a, b):
    return a[0] * b[0] + a[1] * b[1] + a[2] * b[2]


def roe_flux(left, right, n):
    rho_l, u_l, p_l = left[0], left[1:4], left[4]
    rho_r, u_r, p_r = right[0], right[1:4], right[4]
    vn_l, vn_r = dot3(u_l, n), dot3(u_r, n)
    flux_l = physical(left, n, vn_l)
    flux_r = physical(right, n, vn_r)
    root_l, root_r = jnp.sqrt(rho_l), jnp.sqrt(rho_r)
    inverse = 1.0 / (root_l + root_r)
    part_l, part_r = root_l * inverse, root_r * inverse
    rho_a = root_l * root_r
    ratio = GAMMA / (GAMMA - 1.0)
    enth_l = (ratio * p_l + flux_l[5]) / rho_l
    enth_r = (ratio * p_r + flux_r[5]) / rho_r
    u_a = [part_l * a + part_r * b for a, b in zip(u_l, u_r)]
    enth_a = part_l * enth_l + part_r * enth_r
    half_speed = 0.5 * dot3(u_a, u_a)
    sound_sq = (GAMMA - 1.0) * (enth_a - half_speed)
    sound = jnp.sqrt(sound_sq)
    vn_a = dot3(u_a, n)
    d_rho, d_p = rho_r - rho_l, p_r - p_l
    d_u = [b - a for a, b in zip(u_l, u_r)]
    d_vn = dot3(d_u, n)
    per_sq = 1.0 / sound_sq
    slope = rho_a * sound * d_vn
    wave_1 = entropy_fixed(vn_a - sound, sound) * (d_p - slope) * (0.5 * per_sq)
    wave_5 = entropy_fixed(vn_a + sound, sound) * (d_p + slope) * (0.5 * per_sq)
    middle = entropy_fixed(vn_a, sound)
    wave_2 = middle * (d_rho - d_p * per_sq)
    shear = middle * rho_a
    both = wave_1 + wave_5
    total = both + wave_2
    across = sound * (wave_5 - wave_1)
    out = [flux_l[0] + flux_r[0] - total]
    tilt = across - shear * d_vn
    for i in range(3):
        out.append(flux_l[1 + i] + flux_r[1 + i] - (total * u_a[i] + tilt * n[i] + shear * d_u[i]))
    energy = (
        both * enth_a
        + across * vn_a
        + wave_2 * half_speed
        + shear * (dot3(u_a, d_u) - vn_a * d_vn)
    )
    out.append(flux_l[4] + flux_r[4] - energy)
    return out


def floored(w):
    return [jnp.maximum(w[0], FLOOR), w[1], w[2], w[3], jnp.maximum(w[4], FLOOR)]


def polynomials(coefs, side, u, f, basis, part):
    low = iota(0) < 4
    for point in range(2):
        terms = [coefs[r] * basis[side * 2 + point, r % 5, u * 4 + f] for r in range(ROWS)]
        split = {r: (jnp.where(low, terms[r], 0.0), jnp.where(low, 0.0, terms[r])) for r in (2, 7)}
        sums = [
            (terms[0] + terms[1]) + split[2][0],
            (terms[3] + terms[4]) + split[2][1],
            (terms[5] + terms[6]) + split[7][0],
            (terms[8] + terms[9]) + split[7][1],
            (terms[10] + terms[11]) + jnp.where(low, terms[12], 0.0),
        ]
        place = (point * 4 + f) * 8
        for v in range(5):
            part[v, u, place : place + 8, :] = sums[v]


def kernel(
    groups,
    state_h, pinv_h, sten_h, send_h, gids_h, fc_h, fg_h, fb_h,
    out_ref,
    st, pb, sn, sd, gi, fc, fg, fb,
    tbl, snd1, rcv1, snd2, rcv2, snd3, rcv3,
    nidx, ridx, pf, near, ctab, rgat, gtab, bas, bf32, hot, slots, geo,
    part, terms, cen, left_w, turn, wl,
    in_sem, s1, r1, s2, r2,
):
    g = lax.axis_index("group")
    d = lax.axis_index("dom")
    beside = [d + (1 << b) * (1 - 2 * ((d // (1 << b)) % 2)) for b in range(BITS)]
    has_low = g > 0
    has_high = g < groups - 1

    barrier = pltpu.get_barrier_semaphore()
    for b in ORDER:
        pl.semaphore_signal(barrier, inc=1, device_id=(g, beside[b]), device_id_type=MESH)

    @pl.when(has_low)
    def _():
        pl.semaphore_signal(barrier, inc=1, device_id=(g - 1, d), device_id_type=MESH)

    @pl.when(has_high)
    def _():
        pl.semaphore_signal(barrier, inc=1, device_id=(g + 1, d), device_id_type=MESH)

    pairs = [(state_h, st), (send_h, sd), (gids_h, gi), (sten_h, sn), (pinv_h, pb), (fc_h, fc), (fb_h, fb), (fg_h, fg)]
    loads = [pltpu.make_async_copy(a, b, in_sem.at[i]) for i, (a, b) in enumerate(pairs)]
    for load in loads:
        load.start()

    def exchange(near_src, near_dst, far_src, far_dst, send, recv):
        copies = [
            pltpu.make_async_remote_copy(
                src_ref=near_src.at[b],
                dst_ref=near_dst.at[b],
                send_sem=send.at[b],
                recv_sem=recv.at[b],
                device_id=(g, beside[b]),
                device_id_type=MESH,
            )
            for b in range(BITS)
        ]
        up, down = [
            pltpu.make_async_remote_copy(
                src_ref=far_src(i),
                dst_ref=far_dst(i),
                send_sem=send.at[BITS + i],
                recv_sem=recv.at[BITS + i],
                device_id=(g + 1 - 2 * i, d),
                device_id_type=MESH,
            )
            for i in range(2)
        ]
        return copies, up, down

    def start_far(copies, up, down):
        pl.when(has_low)(down.start)
        pl.when(has_high)(up.start)

    def received(copies, up, down, kinds):
        for kind in kinds:
            if kind == "ends":
                pl.when(has_low)(up.wait_recv)
                pl.when(has_high)(down.wait_recv)
            else:
                copies[kind].wait_recv()

    def sent(copies, up, down):
        for copy in copies:
            copy.wait_send()
        pl.when(has_high)(up.wait_send)
        pl.when(has_low)(down.wait_send)

    lane = iota(1)
    lower_half = lane < 64
    quarter = lane >> 5

    for load in loads[:3]:
        load.wait()
    for t in range(CT):
        tbl[t] = jnp.concatenate([st[:, t * 128 : (t + 1) * 128], jnp.zeros((3, 128), F32)], axis=0)
    own = [tbl[t] for t in range(CT)]
    near_ids = []
    for b in range(BITS):
        row = sd[pl.ds(beside[b], 1), :]
        near_ids.append(wide(jnp.concatenate([row, row], axis=1)))
    far_ids = [wide(gi[i : i + 1, :]) for i in range(2)]
    for i, ids in enumerate(near_ids + far_ids):
        snd1[i] = selected(own, ids & 127, ids >> 7, 0, None)

    first = exchange(
        snd1, rcv1, lambda i: snd1.at[BITS + i], lambda i: rcv1.at[BITS + i], s1, r1
    )
    second = exchange(snd2, rcv2, lambda i: snd3.at[i], lambda i: rcv3.at[i], s2, r2)
    pl.semaphore_wait(barrier, BITS + jnp.where(has_low, 1, 0) + jnp.where(has_high, 1, 0))
    first[0][4].start()
    start_far(*first)
    for b in ORDER[1:]:
        first[0][b].start()

    @pl.when(g == 0)
    def _():
        rcv1[BITS] = jnp.zeros((8, 128), F32)
        rcv3[0] = jnp.zeros((7, 8, 128), F32)

    @pl.when(g == groups - 1)
    def _():
        rcv1[BITS + 1] = jnp.zeros((8, 128), F32)
        rcv3[1] = jnp.zeros((7, 8, 128), F32)

    loads[3].wait()

    def own_neighbours(ct):
        for jt in range(JT):
            index = table_index(sn[jt * 8 : jt * 8 + 8, lanes_at(ct)], d)
            nidx[ct, jt] = index
            lanes, tile = index & 127, index >> 7
            for v in range(5):
                tiles = [wide(tbl[t, v : v + 1, :]) for t in range(CT)]
                near[ct, v, jt] = selected(tiles, lanes, tile, 0, None)

    loop(CT, own_neighbours)
    for load in loads[4:]:
        load.wait()

    def widen(ct):
        for k in range(COEF):
            pf[ct, k] = pb[k, :, lanes_at(ct)].astype(F32)

    loop(CT, widen)

    def unpack_basis(ft):
        at = lanes_at(ft)
        bf32[ft] = fb[:, at].astype(F32)
        for i in range(4):
            base = 20 * i
            bas[i, 0, ft] = bf32[ft, base : base + 8, :]
            bas[i, 1, ft] = bf32[ft, base + 8 : base + 16, :]
            bas[i, 2, ft] = jnp.concatenate(
                [bf32[ft, base + 16 : base + 20, :], bf32[ft, base : base + 4, :]], axis=0
            )
            bas[i, 3, ft] = bf32[ft, base + 4 : base + 12, :]
            bas[i, 4, ft] = bf32[ft, base + 12 : base + 20, :]
        cell = lax.broadcasted_iota(I32, (128, 128), 0)
        for e in range(2):
            same = cell == (fc[e : e + 1, at] & 127)
            hot[e * 128 : e * 128 + 128, at] = jnp.where(same, 1.0, 0.0).astype(BF16)
        ridx[ft] = coef_index(wide(fc[1:2, at]), d)

    loop(FT, unpack_basis)

    for ft in range(FT):
        at = slice(ft * 128, ft * 128 + 128)
        for i in range(2):
            row = i * 4 + ft % 4
            for e in range(2):
                slots[e, ft // 4, row : row + 1, :] = fc[e : e + 1, at]
            for e in range(4):
                geo[e, ft // 4, row : row + 1, :] = fg[e : e + 1, at]

    def fill_table(kinds):
        received(*first, kinds)
        if 0 in kinds:
            tbl[6] = jnp.where(lower_half, rcv1[0], rcv1[1])
            tbl[7] = jnp.where(lower_half, rcv1[2], rcv1[3])
        if 4 in kinds:
            tbl[8] = rcv1[4]
        if "ends" in kinds:
            tbl[9] = rcv1[5]
            tbl[10] = rcv1[6]

    fill_table(EARLY)

    def other_neighbours(ct):
        for jt in range(JT):
            index = nidx[ct, jt]
            lanes, tile = index & 127, index >> 7
            for v in range(5):
                acc = near[ct, v, jt]
                for t in tiles_of(EARLY, TABLE_TILES):
                    acc = selected([wide(tbl[t, v : v + 1, :])], lanes, tile, t, acc)
                near[ct, v, jt] = acc

    if EARLY:
        for ct in range(CT):
            other_neighbours(ct)

    fill_table(LATE)

    def coefficients(pair):
        for i in range(6):
            ct = i
            diffs = [[None] * JT for _ in range(5)]
            for jt in range(JT):
                index = nidx[ct, jt]
                lanes, tile = index & 127, index >> 7
                for v in range(5):
                    value = near[ct, v, jt]
                    for t in tiles_of(LATE, TABLE_TILES):
                        value = selected([wide(tbl[t, v : v + 1, :])], lanes, tile, t, value)
                    diff = value - wide(tbl[ct, v : v + 1, :])
                    diffs[v][jt] = diff.astype(BF16).astype(F32)
            for r in range(ROWS):
                for s in range(8):
                    v, k = divmod(8 * r + s, COEF)
                    if v > 4:
                        continue
                    x = [pf[ct, k, jt * 8 : jt * 8 + 8, :] * diffs[v][jt] for jt in range(JT)]
                    terms[i, r, s * 8 : s * 8 + 8, :] = ((x[0] + x[1]) + (x[2] + x[3])) + x[4]
            for r in range(ROWS):
                ctab[r, ct] = row_sums(terms.at[i, r])

    terms[:, ROWS - 1, 32:64, :] = jnp.zeros((6, 32, 128), F32)
    coefficients(0)

    spread = [lane_gather(ids, lane & 31) for ids in near_ids]
    mixed = spread[0]
    for q in range(1, 4):
        mixed = jnp.where(quarter == q, spread[q], mixed)
    turned = [mixed] + [pltpu.roll(mixed, 32 * a, 1) for a in range(1, 4)]
    ends = jnp.where(lower_half, far_ids[0], pltpu.roll(far_ids[1], 64, 1))
    ends = [ends, pltpu.roll(ends, 64, 1)]

    def picked(r, ids):
        return selected([ctab[r, t] for t in range(CT)], ids & 127, ids >> 7, 0, None)

    groups_of = [range(4 * m, min(4 * m + 4, ROWS)) for m in range(4)]
    for m in range(7):
        rows = range(2 * m, min(2 * m + 2, ROWS))
        got = [picked(r, ends[r % 2]) for r in rows]
        snd3[0, m] = jnp.where(lower_half, got[0], got[-1])
        snd3[1, m] = jnp.where(lower_half, got[-1], got[0])
    start_far(*second)
    for m, rows in enumerate(groups_of):
        got = [picked(r, spread[4]) for r in rows]
        mix = got[0]
        for q in range(1, len(got)):
            mix = jnp.where(quarter == q, got[q], mix)
        snd2[4, m] = mix
    second[0][4].start()
    for m, rows in enumerate(groups_of):
        got = [picked(r, turned[r % 4]) for r in rows]
        for b in range(4):
            mix = got[-b % len(got)]
            for q in range(1, len(got)):
                mix = jnp.where(quarter == q, got[(q - b) % 4], mix)
            snd2[b, m] = mix
    for b in ORDER[1:]:
        second[0][b].start()

    def left_side(u):
        for f in range(4):
            slot = wide(fc[0:1, lanes_at(u * 4 + f)])
            lanes, tile = slot & 127, slot >> 7
            coefs = [
                selected([ctab[r, t] for t in range(CT)], lanes, tile, 0, None)
                for r in range(ROWS)
            ]
            polynomials(coefs, 0, u, f, bas, part)

    loop(UT, left_side)

    def right_own(u):
        for f in range(4):
            index = ridx[u * 4 + f]
            lanes, tile = index & 127, index >> 7
            for r in range(ROWS):
                own_part = selected([ctab[r, t] for t in range(CT)], lanes, tile, 0, None)
                rgat[u * 4 + f, r] = own_part

    loop(UT, right_own)

    def centres(u):
        slot = slots[0, u]
        for v in range(5):
            tiles = [wide(tbl[t, v : v + 1, :]) for t in range(CT)]
            centre = selected(tiles, slot & 127, slot >> 7, 0, None)
            left_w[v, u] = centre + row_sums(part.at[v, u])
        index = table_index(slots[1, u], d)
        for v in range(5):
            tiles = [wide(tbl[t, v : v + 1, :]) for t in range(11)]
            cen[v, u] = selected(tiles, index & 127, index >> 7, 0, None)

    loop(UT, centres)

    def fill_ghosts(kinds):
        received(*second, kinds)
        for r in range(ROWS):
            m, a = divmod(r, 4)
            if 0 in kinds:
                mix = rcv2[-a % 4, m]
                for q in range(1, 4):
                    mix = jnp.where(quarter == q, rcv2[(q - a) % 4, m], mix)
                gtab[r, 0] = mix
            if "ends" in kinds:
                gtab[r, 1] = jnp.where(lower_half, rcv3[r % 2, r // 2], rcv3[1 - r % 2, r // 2])

    def ghost_rows(kinds, lanes, tile, r, acc):
        for t in tiles_of(kinds, GHOST_TILES):
            if t == 0:
                acc = selected([gtab[r, 0]], lanes[r % 4], tile, 6, acc)
            elif t == 1:
                acc = selected([gtab[r, 1]], lanes[2 * (r % 2)], tile, 7, acc)
            else:
                acc = selected([rcv2[4, r // 4]], lanes[r % 4], tile, 8, acc)
        return acc

    fill_ghosts(EARLY_COEFS)

    def right_near(u):
        for f in range(4):
            index = ridx[u * 4 + f]
            tile = index >> 7
            lanes = [(index + 32 * a) & 127 for a in range(4)]
            for r in range(ROWS):
                acc = rgat[u * 4 + f, r]
                rgat[u * 4 + f, r] = ghost_rows(EARLY_COEFS, lanes, tile, r, acc)

    if EARLY_COEFS:
        for u in range(UT):
            right_near(u)
    turn[...] = jnp.zeros((UT, 64, 128), F32)
    fill_ghosts(LATE_COEFS)

    for u in range(UT):
        for f in range(4):
            index = ridx[u * 4 + f]
            tile = index >> 7
            lanes = [(index + 32 * a) & 127 for a in range(4)]
            coefs = [
                ghost_rows(LATE_COEFS, lanes, tile, r, rgat[u * 4 + f, r])
                for r in range(ROWS)
            ]
            polynomials(coefs, 1, u, f, bas, part)
    left = floored([left_w[v] for v in range(5)])
    right = []
    for v in range(5):
        sums = [row_sums(part.at[v, u])[None] for u in range(UT)]
        right.append(cen[v] + jnp.concatenate(sums, axis=0))
    flux = roe_flux(left, floored(right), [geo[i] for i in range(3)])
    scale = 0.25 * geo[3]
    for v in range(5):
        weighted = scale * flux[v]
        for u in range(UT):
            turn[u, v * 8 : v * 8 + 8, :] = weighted[u] + pltpu.roll(weighted[u], 4, 0)
    for ft in range(FT):
        at = slice(ft * 128, (ft + 1) * 128)
        whole = turn[ft // 4, pl.ds(ft % 4, 8, stride=8), :]
        high = whole.astype(BF16).astype(F32)
        rest = whole - high
        for e in range(2):
            tile = wide(fc[e : e + 1, at]) >> 7
            for t in range(CT):
                mask = tile == t
                rows = [jnp.where(mask, high, 0.0), jnp.where(mask, rest, 0.0)]
                place = (e * CT + t) * 16
                wl[place : place + 16, at] = jnp.concatenate(rows, axis=0).astype(BF16)
    total = lax.dot_general(
        wl[...], hot[...], (((1,), (1,)), ((), ())), preferred_element_type=F32
    )
    for t in range(CT):
        gained = total[t * 16 : t * 16 + 16, 0:128]
        lost = total[(CT + t) * 16 : (CT + t) * 16 + 16, 128:256]
        change = gained - lost
        out_ref[:, t * 128 : t * 128 + 128] = (change[0:8] + change[8:16])[0:5]
    sent(*first)
    sent(*second)


def per_device(groups, *args):
    any_spec = pl.BlockSpec(memory_space=pl.ANY)
    vmem = pltpu.VMEM
    tile = (8, 128)
    scratch = [
        vmem((5, CELLS), F32),
        vmem((COEF, STEN, CELLS), BF16),
        vmem((STEN, CELLS), I32),
        vmem(args[3].shape, I32),
        vmem((2, 128), I32),
        vmem((2, FACES), I32),
        vmem((4, FACES), F32),
        vmem((80, FACES), BF16),
        vmem((11,) + tile, F32),
        vmem((7,) + tile, F32),
        vmem((7,) + tile, F32),
        vmem((BITS, 4) + tile, F32),
        vmem((BITS, 4) + tile, F32),
        vmem((2, 7) + tile, F32),
        vmem((2, 7) + tile, F32),
        vmem((CT, JT) + tile, I32),
        vmem((FT,) + tile, I32),
        vmem((CT, COEF, STEN, 128), F32),
        vmem((CT, 5, JT) + tile, F32),
        vmem((ROWS, CT) + tile, F32),
        vmem((FT, ROWS) + tile, F32),
        vmem((ROWS, 2) + tile, F32),
        vmem((4, 5, FT) + tile, F32),
        vmem((FT, 80, 128), F32),
        vmem((256, FACES), BF16),
        vmem((2, UT) + tile, I32),
        vmem((4, UT) + tile, F32),
        vmem((5, UT, 64, 128), F32),
        vmem((6, ROWS, 64, 128), F32),
        vmem((5, UT) + tile, F32),
        vmem((5, UT) + tile, F32),
        vmem((UT, 64, 128), F32),
        vmem((192, FACES), BF16),
        pltpu.SemaphoreType.DMA((8,)),
        pltpu.SemaphoreType.DMA((7,)),
        pltpu.SemaphoreType.DMA((7,)),
        pltpu.SemaphoreType.DMA((7,)),
        pltpu.SemaphoreType.DMA((7,)),
    ]
    return pl.pallas_call(
        functools.partial(kernel, groups),
        out_shape=pltpu.VMEM((5, CELLS), F32),
        in_specs=[any_spec] * 8,
        out_specs=pl.BlockSpec(memory_space=pltpu.VMEM),
        scratch_shapes=scratch,
        compiler_params=pltpu.CompilerParams(
            collective_id=0, has_side_effects=True, vmem_limit_bytes=56 * 1024 * 1024
        ),
    )(*args)


def solution(mesh):
    both = ("group", "dom")
    in_specs = (
        P(None, both),
        P(None, None, both),
        P(None, both),
        P(both, None),
        P(both, None),
        P(None, both),
        P(None, both),
        P(None, both),
    )
    return jax.shard_map(
        functools.partial(per_device, mesh.shape["group"]),
        mesh=mesh,
        in_specs=in_specs,
        out_specs=P(None, both),
        check_vma=False,
    )
```

```python
import functools

import jax
import jax.numpy as jnp
from jax import lax
from jax.experimental import pallas as pl
from jax.experimental.pallas import tpu as pltpu
from jax.sharding import PartitionSpec as P

GAMMA = 1.4
FLOOR = 0.2
MESH = pl.DeviceIdType.MESH
F32 = jnp.float32
BF16 = jnp.bfloat16
I32 = jnp.int32

CELLS = 768
FACES = 1536
CT = CELLS // 128
FT = FACES // 128
COEF = 20
STEN = 40
JT = STEN // 8
ROWS = 13
BITS = 5
ORDER = (4, 1, 3, 0, 2)
UT = FT // 4

STATES = (0, 1, 2, 3, 4, "ends")
EARLY_COEFS = (0, 1, 2, 3, 4)
LATE_COEFS = ("ends",)
GHOST_TILES = {0: (0,), 4: (2,), "ends": (1,)}


def tiles_of(kinds, tiles):
    return [t for kind, of in tiles.items() if kind in kinds for t in of]


def loop(count, body):
    def step(i, carry):
        body(i)
        return carry

    lax.fori_loop(0, count, step, 0)


def lanes_at(tile):
    return pl.ds(pl.multiple_of(tile * 128, 128), 128)


def lane_gather(values, lanes):
    return jnp.take_along_axis(values, lanes, axis=1, mode="promise_in_bounds")


def wide(row):
    return jnp.broadcast_to(row, (8, 128))


def iota(axis):
    return lax.broadcasted_iota(I32, (8, 128), axis)


def row_sums(ref):
    x = [ref[pl.ds(j, 8, stride=8), :] for j in range(8)]
    return ((x[0] + x[1]) + (x[2] + x[3])) + ((x[4] + x[5]) + (x[6] + x[7]))


def selected(tiles, lanes, tile, start, acc):
    for i, values in enumerate(tiles):
        got = lane_gather(values, lanes)
        acc = got if acc is None else jnp.where(tile == start + i, got, acc)
    return acc


def table_index(slot, column):
    flip = lax.shift_right_arithmetic(slot - 768, 6) ^ column
    bit = (flip >> 1) - (flip >> 3) - 2 * (flip >> 4)
    near = 768 + bit * 64 + (slot & 63)
    return jnp.where(slot < 768, slot, jnp.where(slot < 2816, near, slot - 1664))


def coef_index(slot, column):
    flip = lax.shift_right_arithmetic(slot - 768, 6) ^ column
    bit = (flip >> 1) - (flip >> 3) - 2 * (flip >> 4)
    near = jnp.where(bit < 4, 768 + bit * 32, 1024) + (slot & 31)
    far = 896 + jnp.where(slot < 2944, 0, 64) + (slot & 63)
    return jnp.where(slot < 768, slot, jnp.where(slot < 2816, near, far))


def packed(tile):
    row = iota(0)
    lowest = jnp.where((row == 0) | (row == 4), 0.6, -0.5)
    steps = ((tile - lowest) * 65535.0 + 0.5).astype(I32)
    second = jnp.where(row == 0, pltpu.roll(steps, 4, 0), pltpu.roll(steps, 7, 0))
    return steps | (second << 16)


def low_half(word):
    return word & 65535


def high_half(word):
    return lax.shift_right_logical(word, 16)


def physical(w, n, vn):
    rho, u, v, q, p = w
    kinetic = 0.5 * rho * (u * u + v * v + q * q)
    mass = rho * vn
    energy = (GAMMA / (GAMMA - 1.0) * p + kinetic) * vn
    return mass, mass * u + p * n[0], mass * v + p * n[1], mass * q + p * n[2], energy, kinetic


def entropy_fixed(eigen, sound):
    delta = 0.1 * sound
    magnitude = jnp.abs(eigen)
    return jnp.where(magnitude < delta, (eigen * eigen + delta * delta) / (2.0 * delta), magnitude)


def dot3(a, b):
    return a[0] * b[0] + a[1] * b[1] + a[2] * b[2]


def roe_flux(left, right, n):
    rho_l, u_l, p_l = left[0], left[1:4], left[4]
    rho_r, u_r, p_r = right[0], right[1:4], right[4]
    vn_l, vn_r = dot3(u_l, n), dot3(u_r, n)
    flux_l = physical(left, n, vn_l)
    flux_r = physical(right, n, vn_r)
    root_l, root_r = jnp.sqrt(rho_l), jnp.sqrt(rho_r)
    inverse = 1.0 / (root_l + root_r)
    part_l, part_r = root_l * inverse, root_r * inverse
    rho_a = root_l * root_r
    ratio = GAMMA / (GAMMA - 1.0)
    enth_l = (ratio * p_l + flux_l[5]) / rho_l
    enth_r = (ratio * p_r + flux_r[5]) / rho_r
    u_a = [part_l * a + part_r * b for a, b in zip(u_l, u_r)]
    enth_a = part_l * enth_l + part_r * enth_r
    half_speed = 0.5 * dot3(u_a, u_a)
    sound_sq = (GAMMA - 1.0) * (enth_a - half_speed)
    sound = jnp.sqrt(sound_sq)
    vn_a = dot3(u_a, n)
    d_rho, d_p = rho_r - rho_l, p_r - p_l
    d_u = [b - a for a, b in zip(u_l, u_r)]
    d_vn = dot3(d_u, n)
    per_sq = 1.0 / sound_sq
    slope = rho_a * sound * d_vn
    wave_1 = entropy_fixed(vn_a - sound, sound) * (d_p - slope) * (0.5 * per_sq)
    wave_5 = entropy_fixed(vn_a + sound, sound) * (d_p + slope) * (0.5 * per_sq)
    middle = entropy_fixed(vn_a, sound)
    wave_2 = middle * (d_rho - d_p * per_sq)
    shear = middle * rho_a
    both = wave_1 + wave_5
    total = both + wave_2
    across = sound * (wave_5 - wave_1)
    out = [flux_l[0] + flux_r[0] - total]
    tilt = across - shear * d_vn
    for i in range(3):
        out.append(flux_l[1 + i] + flux_r[1 + i] - (total * u_a[i] + tilt * n[i] + shear * d_u[i]))
    energy = (
        both * enth_a
        + across * vn_a
        + wave_2 * half_speed
        + shear * (dot3(u_a, d_u) - vn_a * d_vn)
    )
    out.append(flux_l[4] + flux_r[4] - energy)
    return out


def floored(w):
    return [jnp.maximum(w[0], FLOOR), w[1], w[2], w[3], jnp.maximum(w[4], FLOOR)]


def polynomials(coefs, side, u, f, basis, part):
    low = iota(0) < 4
    for point in range(2):
        terms = [coefs[r] * basis[side * 2 + point, r % 5, u * 4 + f] for r in range(ROWS)]
        split = {r: (jnp.where(low, terms[r], 0.0), jnp.where(low, 0.0, terms[r])) for r in (2, 7)}
        sums = [
            (terms[0] + terms[1]) + split[2][0],
            (terms[3] + terms[4]) + split[2][1],
            (terms[5] + terms[6]) + split[7][0],
            (terms[8] + terms[9]) + split[7][1],
            (terms[10] + terms[11]) + jnp.where(low, terms[12], 0.0),
        ]
        place = (point * 4 + f) * 8
        for v in range(5):
            part[v, u, place : place + 8, :] = sums[v]


def kernel(
    groups,
    state_h, pinv_h, sten_h, send_h, gids_h, fc_h, fg_h, fb_h,
    out_ref,
    st, pb, sn, sd, gi, fc, fg, fb,
    tbl, words, snd1, rcv1, snd2, rcv2, snd3, rcv3,
    nidx, ridx, pf, near_words, near, ctab, rgat, gtab, bas, bf32, hot, slots, geo,
    part, terms, cen, left_w, turn, wl,
    in_sem, s1, r1, s2, r2,
):
    g = lax.axis_index("group")
    d = lax.axis_index("dom")
    beside = [d + (1 << b) * (1 - 2 * ((d // (1 << b)) % 2)) for b in range(BITS)]
    has_low = g > 0
    has_high = g < groups - 1

    barrier = pltpu.get_barrier_semaphore()
    for b in ORDER:
        pl.semaphore_signal(barrier, inc=1, device_id=(g, beside[b]), device_id_type=MESH)

    @pl.when(has_low)
    def _():
        pl.semaphore_signal(barrier, inc=1, device_id=(g - 1, d), device_id_type=MESH)

    @pl.when(has_high)
    def _():
        pl.semaphore_signal(barrier, inc=1, device_id=(g + 1, d), device_id_type=MESH)

    pairs = [(state_h, st), (send_h, sd), (gids_h, gi), (sten_h, sn), (pinv_h, pb), (fc_h, fc), (fb_h, fb), (fg_h, fg)]
    loads = [pltpu.make_async_copy(a, b, in_sem.at[i]) for i, (a, b) in enumerate(pairs)]
    for load in loads:
        load.start()

    def exchange(near_src, near_dst, far_src, far_dst, send, recv):
        copies = [
            pltpu.make_async_remote_copy(
                src_ref=near_src.at[b],
                dst_ref=near_dst.at[b],
                send_sem=send.at[b],
                recv_sem=recv.at[b],
                device_id=(g, beside[b]),
                device_id_type=MESH,
            )
            for b in range(BITS)
        ]
        up, down = [
            pltpu.make_async_remote_copy(
                src_ref=far_src(i),
                dst_ref=far_dst(i),
                send_sem=send.at[BITS + i],
                recv_sem=recv.at[BITS + i],
                device_id=(g + 1 - 2 * i, d),
                device_id_type=MESH,
            )
            for i in range(2)
        ]
        return copies, up, down

    def start_far(copies, up, down):
        pl.when(has_low)(down.start)
        pl.when(has_high)(up.start)

    def received(copies, up, down, kinds):
        for kind in kinds:
            if kind == "ends":
                pl.when(has_low)(up.wait_recv)
                pl.when(has_high)(down.wait_recv)
            else:
                copies[kind].wait_recv()

    def sent(copies, up, down):
        for copy in copies:
            copy.wait_send()
        pl.when(has_high)(up.wait_send)
        pl.when(has_low)(down.wait_send)

    lane = iota(1)
    lower_half = lane < 64
    quarter = lane >> 5

    for load in loads[:3]:
        load.wait()
    for t in range(CT):
        tbl[t] = jnp.concatenate([st[:, t * 128 : (t + 1) * 128], jnp.zeros((3, 128), F32)], axis=0)
    own = [tbl[t] for t in range(CT)]
    near_ids = []
    for b in range(BITS):
        row = sd[pl.ds(beside[b], 1), :]
        near_ids.append(wide(jnp.concatenate([row, row], axis=1)))
    far_ids = [wide(gi[i : i + 1, :]) for i in range(2)]
    for i, ids in enumerate(near_ids + far_ids):
        snd1[i] = selected(own, ids & 127, ids >> 7, 0, None)

    first = exchange(
        snd1, rcv1, lambda i: snd1.at[BITS + i], lambda i: rcv1.at[BITS + i], s1, r1
    )
    second = exchange(snd2, rcv2, lambda i: snd3.at[i], lambda i: rcv3.at[i], s2, r2)
    pl.semaphore_wait(barrier, BITS + jnp.where(has_low, 1, 0) + jnp.where(has_high, 1, 0))
    first[0][4].start()
    start_far(*first)
    for b in ORDER[1:]:
        first[0][b].start()

    @pl.when(g == 0)
    def _():
        rcv1[BITS] = jnp.zeros((8, 128), F32)
        rcv3[0] = jnp.zeros((7, 8, 128), F32)

    @pl.when(g == groups - 1)
    def _():
        rcv1[BITS + 1] = jnp.zeros((8, 128), F32)
        rcv3[1] = jnp.zeros((7, 8, 128), F32)

    loads[3].wait()

    for t in range(CT):
        words[t] = packed(tbl[t])

    def own_neighbours(ct):
        for jt in range(JT):
            index = table_index(sn[jt * 8 : jt * 8 + 8, lanes_at(ct)], d)
            nidx[ct, jt] = index
            lanes, tile = index & 127, index >> 7
            for w in range(2):
                tiles = [wide(words[t, w : w + 1, :]) for t in range(CT)]
                near_words[ct, w, jt] = selected(tiles, lanes, tile, 0, None)
            tiles = [wide(tbl[t, 3:4, :]) for t in range(CT)]
            near[ct, jt] = selected(tiles, lanes, tile, 0, None)

    loop(CT, own_neighbours)
    for load in loads[4:]:
        load.wait()

    def widen(ct):
        for k in range(COEF):
            pf[ct, k] = pb[k, :, lanes_at(ct)].astype(F32)

    loop(CT, widen)

    def unpack_basis(ft):
        at = lanes_at(ft)
        bf32[ft] = fb[:, at].astype(F32)
        for i in range(4):
            base = 20 * i
            bas[i, 0, ft] = bf32[ft, base : base + 8, :]
            bas[i, 1, ft] = bf32[ft, base + 8 : base + 16, :]
            bas[i, 2, ft] = jnp.concatenate(
                [bf32[ft, base + 16 : base + 20, :], bf32[ft, base : base + 4, :]], axis=0
            )
            bas[i, 3, ft] = bf32[ft, base + 4 : base + 12, :]
            bas[i, 4, ft] = bf32[ft, base + 12 : base + 20, :]
        cell = lax.broadcasted_iota(I32, (128, 128), 0)
        for e in range(2):
            same = cell == (fc[e : e + 1, at] & 127)
            hot[e * 128 : e * 128 + 128, at] = jnp.where(same, 1.0, 0.0).astype(BF16)
        ridx[ft] = coef_index(wide(fc[1:2, at]), d)

    loop(FT, unpack_basis)

    for ft in range(FT):
        at = slice(ft * 128, ft * 128 + 128)
        for i in range(2):
            row = i * 4 + ft % 4
            for e in range(2):
                slots[e, ft // 4, row : row + 1, :] = fc[e : e + 1, at]
            for e in range(4):
                geo[e, ft // 4, row : row + 1, :] = fg[e : e + 1, at]

    received(*first, STATES)
    tbl[6] = jnp.where(lower_half, rcv1[0], rcv1[1])
    tbl[7] = jnp.where(lower_half, rcv1[2], rcv1[3])
    tbl[8] = rcv1[4]
    tbl[9] = rcv1[5]
    tbl[10] = rcv1[6]
    for t in range(CT, 11):
        words[t] = packed(tbl[t])

    def coefficients(pair):
        for i in range(6):
            ct = i
            diffs = [[None] * JT for _ in range(5)]
            for jt in range(JT):
                index = nidx[ct, jt]
                lanes, tile = index & 127, index >> 7
                for w, (v_low, v_high) in enumerate(((0, 4), (1, 2))):
                    tiles = [wide(words[t, w : w + 1, :]) for t in range(CT, 11)]
                    word = selected(tiles, lanes, tile, CT, near_words[ct, w, jt])
                    mine = wide(words[ct, w : w + 1, :])
                    for v, unpack in ((v_low, low_half), (v_high, high_half)):
                        steps = (unpack(word) - unpack(mine)).astype(F32)
                        diffs[v][jt] = (steps * (1.0 / 65535.0)).astype(BF16).astype(F32)
                tiles = [wide(tbl[t, 3:4, :]) for t in range(CT, 11)]
                value = selected(tiles, lanes, tile, CT, near[ct, jt])
                diffs[3][jt] = (value - wide(tbl[ct, 3:4, :])).astype(BF16).astype(F32)
            for r in range(ROWS):
                for s in range(8):
                    v, k = divmod(8 * r + s, COEF)
                    if v > 4:
                        continue
                    x = [pf[ct, k, jt * 8 : jt * 8 + 8, :] * diffs[v][jt] for jt in range(JT)]
                    terms[i, r, s * 8 : s * 8 + 8, :] = ((x[0] + x[1]) + (x[2] + x[3])) + x[4]
            for r in range(ROWS):
                ctab[r, ct] = row_sums(terms.at[i, r])

    terms[:, ROWS - 1, 32:64, :] = jnp.zeros((6, 32, 128), F32)
    coefficients(0)

    spread = [lane_gather(ids, lane & 31) for ids in near_ids]
    mixed = spread[0]
    for q in range(1, 4):
        mixed = jnp.where(quarter == q, spread[q], mixed)
    turned = [mixed] + [pltpu.roll(mixed, 32 * a, 1) for a in range(1, 4)]
    ends = jnp.where(lower_half, far_ids[0], pltpu.roll(far_ids[1], 64, 1))
    ends = [ends, pltpu.roll(ends, 64, 1)]

    def picked(r, ids):
        return selected([ctab[r, t] for t in range(CT)], ids & 127, ids >> 7, 0, None)

    groups_of = [range(4 * m, min(4 * m + 4, ROWS)) for m in range(4)]
    for m in range(7):
        rows = range(2 * m, min(2 * m + 2, ROWS))
        got = [picked(r, ends[r % 2]) for r in rows]
        snd3[0, m] = jnp.where(lower_half, got[0], got[-1])
        snd3[1, m] = jnp.where(lower_half, got[-1], got[0])
    start_far(*second)
    for m, rows in enumerate(groups_of):
        got = [picked(r, spread[4]) for r in rows]
        mix = got[0]
        for q in range(1, len(got)):
            mix = jnp.where(quarter == q, got[q], mix)
        snd2[4, m] = mix
    second[0][4].start()
    for m, rows in enumerate(groups_of):
        got = [picked(r, turned[r % 4]) for r in rows]
        for b in range(4):
            mix = got[-b % len(got)]
            for q in range(1, len(got)):
                mix = jnp.where(quarter == q, got[(q - b) % 4], mix)
            snd2[b, m] = mix
    for b in ORDER[1:]:
        second[0][b].start()

    def left_side(u):
        for f in range(4):
            slot = wide(fc[0:1, lanes_at(u * 4 + f)])
            lanes, tile = slot & 127, slot >> 7
            coefs = [
                selected([ctab[r, t] for t in range(CT)], lanes, tile, 0, None)
                for r in range(ROWS)
            ]
            polynomials(coefs, 0, u, f, bas, part)

    loop(UT, left_side)

    def right_own(u):
        for f in range(4):
            index = ridx[u * 4 + f]
            lanes, tile = index & 127, index >> 7
            for r in range(ROWS):
                own_part = selected([ctab[r, t] for t in range(CT)], lanes, tile, 0, None)
                rgat[u * 4 + f, r] = own_part

    loop(UT, right_own)

    def centres(u):
        slot = slots[0, u]
        for v in range(5):
            tiles = [wide(tbl[t, v : v + 1, :]) for t in range(CT)]
            centre = selected(tiles, slot & 127, slot >> 7, 0, None)
            left_w[v, u] = centre + row_sums(part.at[v, u])
        index = table_index(slots[1, u], d)
        for v in range(5):
            tiles = [wide(tbl[t, v : v + 1, :]) for t in range(11)]
            cen[v, u] = selected(tiles, index & 127, index >> 7, 0, None)

    loop(UT, centres)

    def fill_ghosts(kinds):
        received(*second, kinds)
        for r in range(ROWS):
            m, a = divmod(r, 4)
            if 0 in kinds:
                mix = rcv2[-a % 4, m]
                for q in range(1, 4):
                    mix = jnp.where(quarter == q, rcv2[(q - a) % 4, m], mix)
                gtab[r, 0] = mix
            if "ends" in kinds:
                gtab[r, 1] = jnp.where(lower_half, rcv3[r % 2, r // 2], rcv3[1 - r % 2, r // 2])

    def ghost_rows(kinds, lanes, tile, r, acc):
        for t in tiles_of(kinds, GHOST_TILES):
            if t == 0:
                acc = selected([gtab[r, 0]], lanes[r % 4], tile, 6, acc)
            elif t == 1:
                acc = selected([gtab[r, 1]], lanes[2 * (r % 2)], tile, 7, acc)
            else:
                acc = selected([rcv2[4, r // 4]], lanes[r % 4], tile, 8, acc)
        return acc

    fill_ghosts(EARLY_COEFS)

    def right_near(u):
        for f in range(4):
            index = ridx[u * 4 + f]
            tile = index >> 7
            lanes = [(index + 32 * a) & 127 for a in range(4)]
            for r in range(ROWS):
                acc = rgat[u * 4 + f, r]
                rgat[u * 4 + f, r] = ghost_rows(EARLY_COEFS, lanes, tile, r, acc)

    if EARLY_COEFS:
        for u in range(UT):
            right_near(u)
    turn[...] = jnp.zeros((UT, 64, 128), F32)
    fill_ghosts(LATE_COEFS)

    for u in range(UT):
        for f in range(4):
            index = ridx[u * 4 + f]
            tile = index >> 7
            lanes = [(index + 32 * a) & 127 for a in range(4)]
            coefs = [
                ghost_rows(LATE_COEFS, lanes, tile, r, rgat[u * 4 + f, r])
                for r in range(ROWS)
            ]
            polynomials(coefs, 1, u, f, bas, part)
    left = floored([left_w[v] for v in range(5)])
    right = []
    for v in range(5):
        sums = [row_sums(part.at[v, u])[None] for u in range(UT)]
        right.append(cen[v] + jnp.concatenate(sums, axis=0))
    flux = roe_flux(left, floored(right), [geo[i] for i in range(3)])
    scale = 0.25 * geo[3]
    for v in range(5):
        weighted = scale * flux[v]
        for u in range(UT):
            turn[u, v * 8 : v * 8 + 8, :] = weighted[u] + pltpu.roll(weighted[u], 4, 0)
    for ft in range(FT):
        at = slice(ft * 128, (ft + 1) * 128)
        whole = turn[ft // 4, pl.ds(ft % 4, 8, stride=8), :]
        high = whole.astype(BF16).astype(F32)
        rest = whole - high
        for e in range(2):
            tile = wide(fc[e : e + 1, at]) >> 7
            for t in range(CT):
                mask = tile == t
                rows = [jnp.where(mask, high, 0.0), jnp.where(mask, rest, 0.0)]
                place = (e * CT + t) * 16
                wl[place : place + 16, at] = jnp.concatenate(rows, axis=0).astype(BF16)
    total = lax.dot_general(
        wl[...], hot[...], (((1,), (1,)), ((), ())), preferred_element_type=F32
    )
    for t in range(CT):
        gained = total[t * 16 : t * 16 + 16, 0:128]
        lost = total[(CT + t) * 16 : (CT + t) * 16 + 16, 128:256]
        change = gained - lost
        out_ref[:, t * 128 : t * 128 + 128] = (change[0:8] + change[8:16])[0:5]
    sent(*first)
    sent(*second)


def per_device(groups, *args):
    any_spec = pl.BlockSpec(memory_space=pl.ANY)
    vmem = pltpu.VMEM
    tile = (8, 128)
    scratch = [
        vmem((5, CELLS), F32),
        vmem((COEF, STEN, CELLS), BF16),
        vmem((STEN, CELLS), I32),
        vmem(args[3].shape, I32),
        vmem((2, 128), I32),
        vmem((2, FACES), I32),
        vmem((4, FACES), F32),
        vmem((80, FACES), BF16),
        vmem((11,) + tile, F32),
        vmem((11,) + tile, I32),
        vmem((7,) + tile, F32),
        vmem((7,) + tile, F32),
        vmem((BITS, 4) + tile, F32),
        vmem((BITS, 4) + tile, F32),
        vmem((2, 7) + tile, F32),
        vmem((2, 7) + tile, F32),
        vmem((CT, JT) + tile, I32),
        vmem((FT,) + tile, I32),
        vmem((CT, COEF, STEN, 128), F32),
        vmem((CT, 2, JT) + tile, I32),
        vmem((CT, JT) + tile, F32),
        vmem((ROWS, CT) + tile, F32),
        vmem((FT, ROWS) + tile, F32),
        vmem((ROWS, 2) + tile, F32),
        vmem((4, 5, FT) + tile, F32),
        vmem((FT, 80, 128), F32),
        vmem((256, FACES), BF16),
        vmem((2, UT) + tile, I32),
        vmem((4, UT) + tile, F32),
        vmem((5, UT, 64, 128), F32),
        vmem((6, ROWS, 64, 128), F32),
        vmem((5, UT) + tile, F32),
        vmem((5, UT) + tile, F32),
        vmem((UT, 64, 128), F32),
        vmem((192, FACES), BF16),
        pltpu.SemaphoreType.DMA((8,)),
        pltpu.SemaphoreType.DMA((7,)),
        pltpu.SemaphoreType.DMA((7,)),
        pltpu.SemaphoreType.DMA((7,)),
        pltpu.SemaphoreType.DMA((7,)),
    ]
    return pl.pallas_call(
        functools.partial(kernel, groups),
        out_shape=pltpu.VMEM((5, CELLS), F32),
        in_specs=[any_spec] * 8,
        out_specs=pl.BlockSpec(memory_space=pltpu.VMEM),
        scratch_shapes=scratch,
        compiler_params=pltpu.CompilerParams(
            collective_id=0, has_side_effects=True, vmem_limit_bytes=56 * 1024 * 1024
        ),
    )(*args)


def solution(mesh):
    both = ("group", "dom")
    in_specs = (
        P(None, both),
        P(None, None, both),
        P(None, both),
        P(both, None),
        P(both, None),
        P(None, both),
        P(None, both),
        P(None, both),
    )
    return jax.shard_map(
        functools.partial(per_device, mesh.shape["group"]),
        mesh=mesh,
        in_specs=in_specs,
        out_specs=P(None, both),
        check_vma=False,
    )
```

```python
import functools

import jax
import jax.numpy as jnp
from jax import lax
from jax.experimental import pallas as pl
from jax.experimental.pallas import tpu as pltpu
from jax.sharding import PartitionSpec as P

GAMMA = 1.4
FLOOR = 0.2
MESH = pl.DeviceIdType.MESH
F32 = jnp.float32
BF16 = jnp.bfloat16
I32 = jnp.int32

CELLS = 768
FACES = 1536
CT = CELLS // 128
FT = FACES // 128
COEF = 20
STEN = 40
JT = STEN // 8
ROWS = 13
BITS = 5
ORDER = (4, 1, 3, 0, 2)
UT = FT // 4

EARLY = ()
LATE = (0, 1, 2, 3, 4, "ends")
EARLY_COEFS = (0, 1, 2, 3, 4)
LATE_COEFS = ("ends",)
TABLE_TILES = {0: (6, 7), 4: (8,), "ends": (9, 10)}
GHOST_TILES = {0: (0,), 4: (2,), "ends": (1,)}


def tiles_of(kinds, tiles):
    return [t for kind, of in tiles.items() if kind in kinds for t in of]


def loop(count, body):
    def step(i, carry):
        body(i)
        return carry

    lax.fori_loop(0, count, step, 0)


def lanes_at(tile):
    return pl.ds(pl.multiple_of(tile * 128, 128), 128)


def lane_gather(values, lanes):
    return jnp.take_along_axis(values, lanes, axis=1, mode="promise_in_bounds")


def wide(row):
    return jnp.broadcast_to(row, (8, 128))


def iota(axis):
    return lax.broadcasted_iota(I32, (8, 128), axis)


def row_sums(ref):
    x = [ref[pl.ds(j, 8, stride=8), :] for j in range(8)]
    return ((x[0] + x[1]) + (x[2] + x[3])) + ((x[4] + x[5]) + (x[6] + x[7]))


def selected(tiles, lanes, tile, start, acc):
    for i, values in enumerate(tiles):
        got = lane_gather(values, lanes)
        acc = got if acc is None else jnp.where(tile == start + i, got, acc)
    return acc


def table_index(slot, column):
    flip = lax.shift_right_arithmetic(slot - 768, 6) ^ column
    bit = (flip >> 1) - (flip >> 3) - 2 * (flip >> 4)
    near = 768 + bit * 64 + (slot & 63)
    return jnp.where(slot < 768, slot, jnp.where(slot < 2816, near, slot - 1664))


def coef_index(slot, column):
    flip = lax.shift_right_arithmetic(slot - 768, 6) ^ column
    bit = (flip >> 1) - (flip >> 3) - 2 * (flip >> 4)
    near = jnp.where(bit < 4, 768 + bit * 32, 1024) + (slot & 31)
    far = 896 + jnp.where(slot < 2944, 0, 64) + (slot & 63)
    return jnp.where(slot < 768, slot, jnp.where(slot < 2816, near, far))


def physical(w, n, vn):
    rho, u, v, q, p = w
    kinetic = 0.5 * rho * (u * u + v * v + q * q)
    mass = rho * vn
    energy = (GAMMA / (GAMMA - 1.0) * p + kinetic) * vn
    return mass, mass * u + p * n[0], mass * v + p * n[1], mass * q + p * n[2], energy, kinetic


def entropy_fixed(eigen, sound):
    delta = 0.1 * sound
    magnitude = jnp.abs(eigen)
    return jnp.where(magnitude < delta, (eigen * eigen + delta * delta) / (2.0 * delta), magnitude)


def dot3(a, b):
    return a[0] * b[0] + a[1] * b[1] + a[2] * b[2]


def roe_flux(left, right, n):
    rho_l, u_l, p_l = left[0], left[1:4], left[4]
    rho_r, u_r, p_r = right[0], right[1:4], right[4]
    vn_l, vn_r = dot3(u_l, n), dot3(u_r, n)
    flux_l = physical(left, n, vn_l)
    flux_r = physical(right, n, vn_r)
    root_l, root_r = jnp.sqrt(rho_l), jnp.sqrt(rho_r)
    inverse = 1.0 / (root_l + root_r)
    part_l, part_r = root_l * inverse, root_r * inverse
    rho_a = root_l * root_r
    ratio = GAMMA / (GAMMA - 1.0)
    enth_l = (ratio * p_l + flux_l[5]) / rho_l
    enth_r = (ratio * p_r + flux_r[5]) / rho_r
    u_a = [part_l * a + part_r * b for a, b in zip(u_l, u_r)]
    enth_a = part_l * enth_l + part_r * enth_r
    half_speed = 0.5 * dot3(u_a, u_a)
    sound_sq = (GAMMA - 1.0) * (enth_a - half_speed)
    sound = jnp.sqrt(sound_sq)
    vn_a = dot3(u_a, n)
    d_rho, d_p = rho_r - rho_l, p_r - p_l
    d_u = [b - a for a, b in zip(u_l, u_r)]
    d_vn = dot3(d_u, n)
    per_sq = 1.0 / sound_sq
    slope = rho_a * sound * d_vn
    wave_1 = entropy_fixed(vn_a - sound, sound) * (d_p - slope) * (0.5 * per_sq)
    wave_5 = entropy_fixed(vn_a + sound, sound) * (d_p + slope) * (0.5 * per_sq)
    middle = entropy_fixed(vn_a, sound)
    wave_2 = middle * (d_rho - d_p * per_sq)
    shear = middle * rho_a
    both = wave_1 + wave_5
    total = both + wave_2
    across = sound * (wave_5 - wave_1)
    out = [flux_l[0] + flux_r[0] - total]
    tilt = across - shear * d_vn
    for i in range(3):
        out.append(flux_l[1 + i] + flux_r[1 + i] - (total * u_a[i] + tilt * n[i] + shear * d_u[i]))
    energy = (
        both * enth_a
        + across * vn_a
        + wave_2 * half_speed
        + shear * (dot3(u_a, d_u) - vn_a * d_vn)
    )
    out.append(flux_l[4] + flux_r[4] - energy)
    return out


def floored(w):
    return [jnp.maximum(w[0], FLOOR), w[1], w[2], w[3], jnp.maximum(w[4], FLOOR)]


def polynomials(coefs, side, u, f, basis, part):
    low = iota(0) < 4
    for point in range(2):
        terms = [coefs[r] * basis[side * 2 + point, r % 5, u * 4 + f] for r in range(ROWS)]
        split = {r: (jnp.where(low, terms[r], 0.0), jnp.where(low, 0.0, terms[r])) for r in (2, 7)}
        sums = [
            (terms[0] + terms[1]) + split[2][0],
            (terms[3] + terms[4]) + split[2][1],
            (terms[5] + terms[6]) + split[7][0],
            (terms[8] + terms[9]) + split[7][1],
            (terms[10] + terms[11]) + jnp.where(low, terms[12], 0.0),
        ]
        place = (point * 4 + f) * 8
        for v in range(5):
            part[v, u, place : place + 8, :] = sums[v]


def kernel(
    groups,
    state_h, pinv_h, sten_h, send_h, gids_h, fc_h, fg_h, fb_h,
    out_ref,
    st, pb, sn, sd, gi, fc, fg, fb,
    tbl, snd1, rcv1, snd2, rcv2, snd3, rcv3,
    nidx, ridx, pf, near, ctab, rgat, gtab, bas, bf32, hot, slots, geo,
    part, terms, cen, left_w, turn, wl,
    in_sem, s1, r1, s2, r2,
):
    g = lax.axis_index("group")
    d = lax.axis_index("dom")
    beside = [d + (1 << b) * (1 - 2 * ((d // (1 << b)) % 2)) for b in range(BITS)]
    has_low = g > 0
    has_high = g < groups - 1

    barrier = pltpu.get_barrier_semaphore()
    for b in ORDER:
        pl.semaphore_signal(barrier, inc=1, device_id=(g, beside[b]), device_id_type=MESH)

    @pl.when(has_low)
    def _():
        pl.semaphore_signal(barrier, inc=1, device_id=(g - 1, d), device_id_type=MESH)

    @pl.when(has_high)
    def _():
        pl.semaphore_signal(barrier, inc=1, device_id=(g + 1, d), device_id_type=MESH)

    pairs = [(state_h, st), (send_h, sd), (gids_h, gi), (sten_h, sn), (pinv_h, pb), (fc_h, fc), (fb_h, fb), (fg_h, fg)]
    loads = [pltpu.make_async_copy(a, b, in_sem.at[i]) for i, (a, b) in enumerate(pairs)]
    for load in loads:
        load.start()

    def exchange(near_src, near_dst, far_src, far_dst, send, recv):
        copies = [
            pltpu.make_async_remote_copy(
                src_ref=near_src.at[b],
                dst_ref=near_dst.at[b],
                send_sem=send.at[b],
                recv_sem=recv.at[b],
                device_id=(g, beside[b]),
                device_id_type=MESH,
            )
            for b in range(BITS)
        ]
        up, down = [
            pltpu.make_async_remote_copy(
                src_ref=far_src(i),
                dst_ref=far_dst(i),
                send_sem=send.at[BITS + i],
                recv_sem=recv.at[BITS + i],
                device_id=(g + 1 - 2 * i, d),
                device_id_type=MESH,
            )
            for i in range(2)
        ]
        return copies, up, down

    def start_far(copies, up, down):
        pl.when(has_low)(down.start)
        pl.when(has_high)(up.start)

    def received(copies, up, down, kinds):
        for kind in kinds:
            if kind == "ends":
                pl.when(has_low)(up.wait_recv)
                pl.when(has_high)(down.wait_recv)
            else:
                copies[kind].wait_recv()

    def sent(copies, up, down):
        for copy in copies:
            copy.wait_send()
        pl.when(has_high)(up.wait_send)
        pl.when(has_low)(down.wait_send)

    lane = iota(1)
    lower_half = lane < 64
    quarter = lane >> 5

    for load in loads[:3]:
        load.wait()
    for t in range(CT):
        tbl[t] = jnp.concatenate([st[:, t * 128 : (t + 1) * 128], jnp.zeros((3, 128), F32)], axis=0)
    own = [tbl[t] for t in range(CT)]
    near_ids = []
    for b in range(BITS):
        row = sd[pl.ds(beside[b], 1), :]
        near_ids.append(wide(jnp.concatenate([row, row], axis=1)))
    far_ids = [wide(gi[i : i + 1, :]) for i in range(2)]
    for i, ids in enumerate(near_ids + far_ids):
        snd1[i] = selected(own, ids & 127, ids >> 7, 0, None)

    first = exchange(
        snd1, rcv1, lambda i: snd1.at[BITS + i], lambda i: rcv1.at[BITS + i], s1, r1
    )
    second = exchange(snd2, rcv2, lambda i: snd3.at[i], lambda i: rcv3.at[i], s2, r2)
    pl.semaphore_wait(barrier, BITS + jnp.where(has_low, 1, 0) + jnp.where(has_high, 1, 0))
    first[0][4].start()
    start_far(*first)
    for b in ORDER[1:]:
        first[0][b].start()

    @pl.when(g == 0)
    def _():
        rcv1[BITS] = jnp.zeros((8, 128), F32)
        rcv3[0] = jnp.zeros((7, 8, 128), F32)

    @pl.when(g == groups - 1)
    def _():
        rcv1[BITS + 1] = jnp.zeros((8, 128), F32)
        rcv3[1] = jnp.zeros((7, 8, 128), F32)

    loads[3].wait()

    def own_neighbours(ct):
        for jt in range(JT):
            index = table_index(sn[jt * 8 : jt * 8 + 8, lanes_at(ct)], d)
            nidx[ct, jt] = index
            lanes, tile = index & 127, index >> 7
            for v in range(5):
                tiles = [wide(tbl[t, v : v + 1, :]) for t in range(CT)]
                near[ct, v, jt] = selected(tiles, lanes, tile, 0, None)

    loop(CT, own_neighbours)
    for load in loads[4:]:
        load.wait()

    def widen(ct):
        for k in range(COEF):
            pf[ct, k] = pb[k, :, lanes_at(ct)].astype(F32)

    loop(CT, widen)

    def unpack_basis(ft):
        at = lanes_at(ft)
        bf32[ft] = fb[:, at].astype(F32)
        for i in range(4):
            base = 20 * i
            bas[i, 0, ft] = bf32[ft, base : base + 8, :]
            bas[i, 1, ft] = bf32[ft, base + 8 : base + 16, :]
            bas[i, 2, ft] = jnp.concatenate(
                [bf32[ft, base + 16 : base + 20, :], bf32[ft, base : base + 4, :]], axis=0
            )
            bas[i, 3, ft] = bf32[ft, base + 4 : base + 12, :]
            bas[i, 4, ft] = bf32[ft, base + 12 : base + 20, :]
        cell = lax.broadcasted_iota(I32, (128, 128), 0)
        for e in range(2):
            same = cell == (fc[e : e + 1, at] & 127)
            hot[e * 128 : e * 128 + 128, at] = jnp.where(same, 1.0, 0.0).astype(BF16)
        ridx[ft] = coef_index(wide(fc[1:2, at]), d)

    loop(FT, unpack_basis)

    for ft in range(FT):
        at = slice(ft * 128, ft * 128 + 128)
        for i in range(2):
            row = i * 4 + ft % 4
            for e in range(2):
                slots[e, ft // 4, row : row + 1, :] = fc[e : e + 1, at]
            for e in range(4):
                geo[e, ft // 4, row : row + 1, :] = fg[e : e + 1, at]

    def fill_table(kinds):
        received(*first, kinds)
        if 0 in kinds:
            tbl[6] = jnp.where(lower_half, rcv1[0], rcv1[1])
            tbl[7] = jnp.where(lower_half, rcv1[2], rcv1[3])
        if 4 in kinds:
            tbl[8] = rcv1[4]
        if "ends" in kinds:
            tbl[9] = rcv1[5]
            tbl[10] = rcv1[6]

    fill_table(EARLY)

    def other_neighbours(ct):
        for jt in range(JT):
            index = nidx[ct, jt]
            lanes, tile = index & 127, index >> 7
            for v in range(5):
                acc = near[ct, v, jt]
                for t in tiles_of(EARLY, TABLE_TILES):
                    acc = selected([wide(tbl[t, v : v + 1, :])], lanes, tile, t, acc)
                near[ct, v, jt] = acc

    if EARLY:
        for ct in range(CT):
            other_neighbours(ct)

    fill_table(LATE)

    def coefficients(pair):
        for i in range(6):
            ct = i
            diffs = [[None] * JT for _ in range(5)]
            for jt in range(JT):
                index = nidx[ct, jt]
                lanes, tile = index & 127, index >> 7
                for v in range(5):
                    value = near[ct, v, jt]
                    for t in tiles_of(LATE, TABLE_TILES):
                        value = selected([wide(tbl[t, v : v + 1, :])], lanes, tile, t, value)
                    diff = value - wide(tbl[ct, v : v + 1, :])
                    diffs[v][jt] = diff.astype(BF16).astype(F32)
            for r in range(ROWS):
                for s in range(8):
                    v, k = divmod(8 * r + s, COEF)
                    if v > 4:
                        continue
                    x = [pf[ct, k, jt * 8 : jt * 8 + 8, :] * diffs[v][jt] for jt in range(JT)]
                    terms[i, r, s * 8 : s * 8 + 8, :] = ((x[0] + x[1]) + (x[2] + x[3])) + x[4]
            for r in range(ROWS):
                ctab[r, ct] = row_sums(terms.at[i, r])

    terms[:, ROWS - 1, 32:64, :] = jnp.zeros((6, 32, 128), F32)
    coefficients(0)

    spread = [lane_gather(ids, lane & 31) for ids in near_ids]
    mixed = spread[0]
    for q in range(1, 4):
        mixed = jnp.where(quarter == q, spread[q], mixed)
    turned = [mixed] + [pltpu.roll(mixed, 32 * a, 1) for a in range(1, 4)]
    ends = jnp.where(lower_half, far_ids[0], pltpu.roll(far_ids[1], 64, 1))
    ends = [ends, pltpu.roll(ends, 64, 1)]

    def picked(r, ids):
        return selected([ctab[r, t] for t in range(CT)], ids & 127, ids >> 7, 0, None)

    groups_of = [range(4 * m, min(4 * m + 4, ROWS)) for m in range(4)]
    for m in range(7):
        rows = range(2 * m, min(2 * m + 2, ROWS))
        got = [picked(r, ends[r % 2]) for r in rows]
        snd3[0, m] = jnp.where(lower_half, got[0], got[-1])
        snd3[1, m] = jnp.where(lower_half, got[-1], got[0])
    start_far(*second)
    for m, rows in enumerate(groups_of):
        got = [picked(r, spread[4]) for r in rows]
        mix = got[0]
        for q in range(1, len(got)):
            mix = jnp.where(quarter == q, got[q], mix)
        snd2[4, m] = mix
    second[0][4].start()
    for m, rows in enumerate(groups_of):
        got = [picked(r, turned[r % 4]) for r in rows]
        for b in range(4):
            mix = got[-b % len(got)]
            for q in range(1, len(got)):
                mix = jnp.where(quarter == q, got[(q - b) % 4], mix)
            snd2[b, m] = mix
    for b in ORDER[1:]:
        second[0][b].start()

    def left_side(u):
        for f in range(4):
            slot = wide(fc[0:1, lanes_at(u * 4 + f)])
            lanes, tile = slot & 127, slot >> 7
            coefs = [
                selected([ctab[r, t] for t in range(CT)], lanes, tile, 0, None)
                for r in range(ROWS)
            ]
            polynomials(coefs, 0, u, f, bas, part)

    loop(UT, left_side)

    def right_own(u):
        for f in range(4):
            index = ridx[u * 4 + f]
            lanes, tile = index & 127, index >> 7
            for r in range(ROWS):
                own_part = selected([ctab[r, t] for t in range(CT)], lanes, tile, 0, None)
                rgat[u * 4 + f, r] = own_part

    loop(UT, right_own)

    def centres(u):
        slot = slots[0, u]
        for v in range(5):
            tiles = [wide(tbl[t, v : v + 1, :]) for t in range(CT)]
            centre = selected(tiles, slot & 127, slot >> 7, 0, None)
            left_w[v, u] = centre + row_sums(part.at[v, u])
        index = table_index(slots[1, u], d)
        for v in range(5):
            tiles = [wide(tbl[t, v : v + 1, :]) for t in range(11)]
            cen[v, u] = selected(tiles, index & 127, index >> 7, 0, None)

    loop(UT, centres)

    def fill_ghosts(kinds):
        received(*second, kinds)
        for r in range(ROWS):
            m, a = divmod(r, 4)
            if 0 in kinds:
                mix = rcv2[-a % 4, m]
                for q in range(1, 4):
                    mix = jnp.where(quarter == q, rcv2[(q - a) % 4, m], mix)
                gtab[r, 0] = mix
            if "ends" in kinds:
                gtab[r, 1] = jnp.where(lower_half, rcv3[r % 2, r // 2], rcv3[1 - r % 2, r // 2])

    def ghost_rows(kinds, lanes, tile, r, acc):
        for t in tiles_of(kinds, GHOST_TILES):
            if t == 0:
                acc = selected([gtab[r, 0]], lanes[r % 4], tile, 6, acc)
            elif t == 1:
                acc = selected([gtab[r, 1]], lanes[2 * (r % 2)], tile, 7, acc)
            else:
                acc = selected([rcv2[4, r // 4]], lanes[r % 4], tile, 8, acc)
        return acc

    fill_ghosts(EARLY_COEFS)

    def right_near(u):
        for f in range(4):
            index = ridx[u * 4 + f]
            tile = index >> 7
            lanes = [(index + 32 * a) & 127 for a in range(4)]
            for r in range(ROWS):
                acc = rgat[u * 4 + f, r]
                rgat[u * 4 + f, r] = ghost_rows(EARLY_COEFS, lanes, tile, r, acc)

    if EARLY_COEFS:
        for u in range(UT):
            right_near(u)
    turn[...] = jnp.zeros((UT, 64, 128), F32)
    fill_ghosts(LATE_COEFS)

    for u in range(UT):
        for f in range(4):
            index = ridx[u * 4 + f]
            tile = index >> 7
            lanes = [(index + 32 * a) & 127 for a in range(4)]
            coefs = [
                ghost_rows(LATE_COEFS, lanes, tile, r, rgat[u * 4 + f, r])
                for r in range(ROWS)
            ]
            polynomials(coefs, 1, u, f, bas, part)
    left = floored([left_w[v] for v in range(5)])
    right = []
    for v in range(5):
        sums = [row_sums(part.at[v, u])[None] for u in range(UT)]
        right.append(cen[v] + jnp.concatenate(sums, axis=0))
    flux = roe_flux(left, floored(right), [geo[i] for i in range(3)])
    scale = 0.25 * geo[3]
    for v in range(5):
        weighted = scale * flux[v]
        for u in range(UT):
            turn[u, v * 8 : v * 8 + 8, :] = weighted[u] + pltpu.roll(weighted[u], 4, 0)
    for ft in range(FT):
        at = slice(ft * 128, (ft + 1) * 128)
        whole = turn[ft // 4, pl.ds(ft % 4, 8, stride=8), :]
        high = whole.astype(BF16).astype(F32)
        rest = whole - high
        for e in range(2):
            tile = wide(fc[e : e + 1, at]) >> 7
            for t in range(CT):
                mask = tile == t
                rows = [jnp.where(mask, high, 0.0), jnp.where(mask, rest, 0.0)]
                place = (e * CT + t) * 16
                wl[place : place + 16, at] = jnp.concatenate(rows, axis=0).astype(BF16)
        if ft % 4 == 3:
            at = slice((ft - 3) * 128, (ft + 1) * 128)
            summed = lax.dot_general(
                wl[:, at], hot[:, at], (((1,), (1,)), ((), ())), preferred_element_type=F32
            )
            total = summed if ft == 3 else total + summed
    for t in range(CT):
        gained = total[t * 16 : t * 16 + 16, 0:128]
        lost = total[(CT + t) * 16 : (CT + t) * 16 + 16, 128:256]
        change = gained - lost
        out_ref[:, t * 128 : t * 128 + 128] = (change[0:8] + change[8:16])[0:5]
    sent(*first)
    sent(*second)


def per_device(groups, *args):
    any_spec = pl.BlockSpec(memory_space=pl.ANY)
    vmem = pltpu.VMEM
    tile = (8, 128)
    scratch = [
        vmem((5, CELLS), F32),
        vmem((COEF, STEN, CELLS), BF16),
        vmem((STEN, CELLS), I32),
        vmem(args[3].shape, I32),
        vmem((2, 128), I32),
        vmem((2, FACES), I32),
        vmem((4, FACES), F32),
        vmem((80, FACES), BF16),
        vmem((11,) + tile, F32),
        vmem((7,) + tile, F32),
        vmem((7,) + tile, F32),
        vmem((BITS, 4) + tile, F32),
        vmem((BITS, 4) + tile, F32),
        vmem((2, 7) + tile, F32),
        vmem((2, 7) + tile, F32),
        vmem((CT, JT) + tile, I32),
        vmem((FT,) + tile, I32),
        vmem((CT, COEF, STEN, 128), F32),
        vmem((CT, 5, JT) + tile, F32),
        vmem((ROWS, CT) + tile, F32),
        vmem((FT, ROWS) + tile, F32),
        vmem((ROWS, 2) + tile, F32),
        vmem((4, 5, FT) + tile, F32),
        vmem((FT, 80, 128), F32),
        vmem((256, FACES), BF16),
        vmem((2, UT) + tile, I32),
        vmem((4, UT) + tile, F32),
        vmem((5, UT, 64, 128), F32),
        vmem((6, ROWS, 64, 128), F32),
        vmem((5, UT) + tile, F32),
        vmem((5, UT) + tile, F32),
        vmem((UT, 64, 128), F32),
        vmem((192, FACES), BF16),
        pltpu.SemaphoreType.DMA((8,)),
        pltpu.SemaphoreType.DMA((7,)),
        pltpu.SemaphoreType.DMA((7,)),
        pltpu.SemaphoreType.DMA((7,)),
        pltpu.SemaphoreType.DMA((7,)),
    ]
    return pl.pallas_call(
        functools.partial(kernel, groups),
        out_shape=pltpu.VMEM((5, CELLS), F32),
        in_specs=[any_spec] * 8,
        out_specs=pl.BlockSpec(memory_space=pltpu.VMEM),
        scratch_shapes=scratch,
        compiler_params=pltpu.CompilerParams(
            collective_id=0, has_side_effects=True, vmem_limit_bytes=56 * 1024 * 1024
        ),
    )(*args)


def solution(mesh):
    both = ("group", "dom")
    in_specs = (
        P(None, both),
        P(None, None, both),
        P(None, both),
        P(both, None),
        P(both, None),
        P(None, both),
        P(None, both),
        P(None, both),
    )
    return jax.shard_map(
        functools.partial(per_device, mesh.shape["group"]),
        mesh=mesh,
        in_specs=in_specs,
        out_specs=P(None, both),
        check_vma=False,
    )
```
